32 devices in a mesh: dp: 8 (over z, core), fsdp: 4 (over y, x).
Axes of the slice: x: 2, y: 2, z: 4, core: 2. Of those that a mesh axis runs over, the one named last changes fastest.
Arguments:
- activations: bfloat16 [1, 8192, 8192], P(None, 'dp', 'fsdp'), may hold values from -6 to 6
- out_grads: bfloat16 [1, 8192, 22016], P(None, 'dp', 'fsdp'), may hold values from -3 to 3
- projector: bfloat16 [1, 8192, 1024], P(None, 'fsdp'), may hold values from -0.046875 to 0.046875
- first_moment: float32 [1, 22016, 1024], P(None, ('fsdp', 'dp')), may hold values from -16 to 16
- second_moment: float32 [1, 22016, 1024], P(None, ('fsdp', 'dp')), may hold values from 0.05 to 2
Outputs:
- weight_update: float32 [1, 4, 5504, 8192], P(None, None, 'dp', 'fsdp')
- first_new: float32 [1, 22016, 1024], P(None, ('fsdp', 'dp'))
- second_new: float32 [1, 22016, 1024], P(None, ('fsdp', 'dp'))
The draws below stay inside these ranges and needn't reach their ends.
All inputs are finite; a program needn't handle non-finite values.
Results may differ from the reference program's by a relative error of at most 0.018.
Values may be sent and summed in bfloat16 or wider, within the bound.
No kernel may reach another device: no remote copies, remote signals or barrier semaphores. Data moves between devices by JAX's collectives and lax.ppermute only.
A program may use at most 128 MiB of HBM per device.

```python
import math
import jax
import jax.numpy as jnp
from jax import lax

D = 8192
FF = 22016
RANK = 1024
LAYERS = 1
TOK_DEV = 1024
TOKENS = 8192
N_DP = 8
N_FSDP = 4


def with_spikes(entries, rng, source, target, shards_of, factor):
    def block_of(axis_at):
        return (jnp.arange(entries.shape[axis_at]) // (entries.shape[axis_at] // shards_of)).reshape((-1,) + (1,) * (entries.ndim - 1 - axis_at))

    one_side = jax.random.permutation(rng, shards_of)[block_of(target)]
    other_side = (block_of(target) + shards_of // 2) % shards_of
    return jnp.where((block_of(source) == one_side) | (block_of(source) == other_side), factor * entries, entries)


def levels(own_key, dims, split, smallest, high):
    loudness, own = 1.0, jax.random.fold_in(own_key, 6)
    for position, shards_of in split:
        heights = jnp.exp(jax.random.uniform(jax.random.fold_in(own, position), (shards_of,), jnp.float32, smallest / len(split), high / len(split)))
        loudness = loudness * jnp.repeat(heights, dims[position] // shards_of).reshape([-1 if axis == position else 1 for axis in range(len(dims))])
    return loudness


def centred(key, dims, spread, limit, pieces=(), kind=jnp.bfloat16):
    entries = jax.random.normal(key, dims, jnp.float32) * spread
    if len(pieces) > 0:
        entries = levels(key, dims, pieces, -0.22, 0.18) * entries
    return jnp.clip(entries, min=-limit, max=limit).astype(kind)


def bell_draw_with(own_key, shape, deviation, most, cuts, heavy, held_as=jnp.bfloat16):
    values = deviation * jax.random.normal(own_key, shape, jnp.float32)
    if cuts:
        values = values * levels(own_key, shape, cuts, -0.22, 0.18)
    return jnp.clip(with_spikes(values, jax.random.fold_in(own_key, 3), *heavy), -most, most).astype(held_as)


def setup_inputs(seed: int = 0) -> dict:
    splits = jax.random.split(jax.random.key(seed), 6)
    return {
        "activations": centred(splits[0], (LAYERS, TOKENS, D), 1.0, 6.0, ((1, 8), (2, 4))),
        "out_grads": bell_draw_with(splits[1], (LAYERS, TOKENS, FF), (14.0 * TOKENS ** -0.5), 3.0, ((1, 8), (2, 4)), (1, 2, 8, 2.0)),
        "projector": centred(splits[2], (LAYERS, D, RANK), (16 * RANK) ** -0.5, 0.046875, ((1, 4),)),
        "first_moment": centred(splits[3], (LAYERS, FF, RANK), 3.0, 16.0, ((1, 32),), jnp.float32),
        "second_moment": jnp.clip(jnp.exp(math.log(2.0) - 3.6888794 * jax.random.uniform(splits[4], (LAYERS, FF, RANK), jnp.float32) ** levels(splits[4], (LAYERS, FF, RANK), ((1, 32),), -0.2, 0.2)), 0.05, 2.0),
    }


beta_first = 0.9
beta_second = 0.999
adam_count = 100.0
epsilon = 1e-08

def low_rank_gradient(projected, grads):
    blocks_proj = projected.reshape(N_DP, TOK_DEV, RANK)
    blocks_grad = grads.reshape(N_DP, TOK_DEV, FF)

    def accumulate(total, pair):
        term = jnp.dot(pair[1].T, pair[0], preferred_element_type=jnp.float32)
        rounded = lax.optimization_barrier(term.astype(jnp.bfloat16))
        return (total + rounded.astype(jnp.float32), None)
    total, unused = lax.scan(accumulate, jnp.zeros((FF, RANK), jnp.float32), (blocks_proj, blocks_grad))
    return total

def adam_direction(grad_low, first, second):
    first_next = beta_first * first + (1.0 - beta_first) * grad_low
    second_next = beta_second * second + (1.0 - beta_second) * grad_low * grad_low
    bias_first = 1.0 - beta_first ** adam_count
    bias_second = 1.0 - beta_second ** adam_count
    direction = first_next / bias_first / (jnp.sqrt(second_next / bias_second) + epsilon)
    return (first_next, second_next, direction.astype(jnp.bfloat16))

def reference(activations, out_grads, projector, first_moment, second_moment):
    updates = []
    firsts = []
    seconds = []
    for layer_index in range(LAYERS):
        projected = jnp.dot(activations[layer_index], projector[layer_index], preferred_element_type=jnp.float32).astype(jnp.bfloat16)
        grad_low = low_rank_gradient(projected, out_grads[layer_index])
        first_next, second_next, direction = adam_direction(grad_low, first_moment[layer_index], second_moment[layer_index])
        update = jnp.dot(direction, projector[layer_index].T, preferred_element_type=jnp.float32)
        updates.append(update.reshape(N_FSDP, FF // N_FSDP, D))
        firsts.append(first_next)
        seconds.append(second_next)
    return (jnp.stack(updates), jnp.stack(firsts), jnp.stack(seconds))
```

```python
import functools

import jax
import jax.numpy as jnp
from jax import lax
from jax.experimental import pallas as pl
from jax.experimental.pallas import tpu as pltpu
from jax.sharding import PartitionSpec as P

beta_first = 0.9
beta_second = 0.999
adam_count = 100.0
epsilon = 1e-08

F32 = jnp.float32
BF16 = jnp.bfloat16
VMEM_LIMIT = 56 * 1024 * 1024
PARTS = 4


def project(features, basis, order, part, width):
    tokens, depth = features.shape
    count = order.shape[0]
    rows = tokens // count

    def kernel(order_ref, features_ref, basis_ref, *out_refs):
        value = jnp.dot(features_ref[...], basis_ref[...], preferred_element_type=F32).astype(BF16)
        for index, out_ref in enumerate(out_refs):

            @pl.when(pl.program_id(0) == index)
            def _(out_ref=out_ref):
                out_ref[...] = value

    return pl.pallas_call(
        kernel,
        out_shape=[jax.ShapeDtypeStruct((rows, width), BF16)] * count,
        grid_spec=pltpu.PrefetchScalarGridSpec(
            num_scalar_prefetch=1,
            grid=(count,),
            in_specs=[
                pl.BlockSpec((rows, depth), lambda i, order_ref: (order_ref[i], 0)),
                pl.BlockSpec((depth, width), lambda i, order_ref: (0, part)),
            ],
            out_specs=[pl.BlockSpec((rows, width), lambda i, order_ref: (0, 0))] * count,
        ),
        compiler_params=pltpu.CompilerParams(vmem_limit_bytes=VMEM_LIMIT),
        cost_estimate=pl.CostEstimate(
            flops=2 * tokens * depth * width,
            bytes_accessed=2 * (tokens * depth + depth * width + tokens * width),
            transcendentals=0,
        ),
        name="project",
    )(order, features, basis)


def gradient(grads_t, pieces, order, owners):
    _, owned, tokens = grads_t.shape
    rows, width = pieces[0].shape
    count = owners.shape[0]

    def kernel(order_ref, owners_ref, grads_ref, *refs):
        piece_refs, (out_ref, whole_ref) = refs[:-2], refs[-2:]

        @pl.when(pl.program_id(0) == 0)
        def _():
            for index, piece_ref in enumerate(piece_refs):
                start = pl.multiple_of(order_ref[index] * rows, rows)
                whole_ref[pl.ds(start, rows), :] = piece_ref[...]

        out_ref[0] = jnp.dot(grads_ref[0], whole_ref[...], preferred_element_type=F32).astype(BF16)

    return pl.pallas_call(
        kernel,
        out_shape=jax.ShapeDtypeStruct((count, owned, width), BF16),
        grid_spec=pltpu.PrefetchScalarGridSpec(
            num_scalar_prefetch=2,
            grid=(count,),
            in_specs=[pl.BlockSpec((1, owned, tokens), lambda i, order_ref, owners_ref: (owners_ref[i], 0, 0))]
            + [pl.BlockSpec((rows, width), lambda i, order_ref, owners_ref: (0, 0))] * len(pieces),
            out_specs=pl.BlockSpec((1, owned, width), lambda i, order_ref, owners_ref: (i, 0, 0)),
            scratch_shapes=[pltpu.VMEM((tokens, width), BF16)],
        ),
        compiler_params=pltpu.CompilerParams(vmem_limit_bytes=VMEM_LIMIT),
        cost_estimate=pl.CostEstimate(
            flops=2 * count * owned * tokens * width,
            bytes_accessed=2 * (count * owned * tokens + tokens * width + count * owned * width),
            transcendentals=0,
        ),
        name="gradient",
    )(order, owners, grads_t, *pieces)


def adam(arrived, own, other, first, second, held, part):
    owned, rank = first.shape
    width = arrived.shape[1]
    last = own.shape[0] - 1

    def kernel(arrived_ref, own_ref, other_ref, first_ref, second_ref, *refs):
        first_out, second_out, direction_out = refs[-3:]
        grad_low = arrived_ref[...].astype(F32) + own_ref[0].astype(F32) + other_ref[0].astype(F32)
        first_next = beta_first * first_ref[...] + (1.0 - beta_first) * grad_low
        second_next = beta_second * second_ref[...] + (1.0 - beta_second) * grad_low * grad_low
        first_out[...] = first_next
        second_out[...] = second_next
        bias_first = 1.0 - beta_first**adam_count
        bias_second = 1.0 - beta_second**adam_count
        direction = first_next / bias_first / (jnp.sqrt(second_next / bias_second) + epsilon)
        direction_out[...] = direction.astype(BF16)

    column = pl.BlockSpec((owned, width), lambda i: (0, part))
    return pl.pallas_call(
        kernel,
        grid=(1,),
        out_shape=[
            jax.ShapeDtypeStruct((owned, rank), F32),
            jax.ShapeDtypeStruct((owned, rank), F32),
            jax.ShapeDtypeStruct((owned, width), BF16),
        ],
        in_specs=[
            pl.BlockSpec((owned, width), lambda i: (0, 0)),
            pl.BlockSpec((1, owned, width), lambda i: (last, 0, 0)),
            pl.BlockSpec((1, owned, width), lambda i: (last, 0, 0)),
            column,
            column,
        ]
        + [pl.BlockSpec(memory_space=pl.ANY)] * len(held),
        out_specs=[column, column, pl.BlockSpec((owned, width), lambda i: (0, 0))],
        input_output_aliases={5 + index: index for index in range(len(held))},
        compiler_params=pltpu.CompilerParams(vmem_limit_bytes=VMEM_LIMIT),
        cost_estimate=pl.CostEstimate(
            flops=12 * owned * width, bytes_accessed=24 * owned * width, transcendentals=owned * width
        ),
        name="adam",
    )(arrived, own, other, first, second, *held)


def expand(directions, basis, target, held, count):
    owned, width = directions[0].shape
    features, rank = basis.shape
    block = min(512, features)

    def kernel(target_ref, basis_ref, *refs):
        direction_refs, out_ref = refs[: len(directions)], refs[-1]
        total = None
        for index, direction_ref in enumerate(direction_refs):
            term = lax.dot_general(
                direction_ref[...],
                basis_ref[:, index * width : (index + 1) * width],
                (((1,), (1,)), ((), ())),
                preferred_element_type=F32,
            )
            total = term if total is None else total + term
        out_ref[0] = total

    return pl.pallas_call(
        kernel,
        out_shape=jax.ShapeDtypeStruct((count, owned, features), F32),
        grid_spec=pltpu.PrefetchScalarGridSpec(
            num_scalar_prefetch=1,
            grid=(features // block,),
            in_specs=[pl.BlockSpec((block, rank), lambda i, target_ref: (i, 0))]
            + [pl.BlockSpec((owned, width), lambda i, target_ref: (0, 0))] * len(directions)
            + [pl.BlockSpec(memory_space=pl.ANY)] * len(held),
            out_specs=pl.BlockSpec((1, owned, block), lambda i, target_ref: (target_ref[0], 0, i)),
        ),
        input_output_aliases={2 + len(directions): 0} if held else {},
        compiler_params=pltpu.CompilerParams(vmem_limit_bytes=VMEM_LIMIT),
        cost_estimate=pl.CostEstimate(
            flops=2 * owned * rank * features,
            bytes_accessed=2 * (owned * rank + rank * features) + 4 * owned * features,
            transcendentals=0,
        ),
        name="expand",
    )(target, basis, *directions, *held)


def total_of(terms):
    total = terms[0].astype(F32)
    for term in terms[1:]:
        total = total + term.astype(F32)
    return total.astype(BF16)


def local(activations, out_grads, projector, first_moment, second_moment):
    owned = first_moment.shape[1]
    features = activations[0]
    basis = projector[0]
    rank = basis.shape[1]
    tokens = features.shape[0]
    dp_count, fsdp_count = lax.axis_size("dp"), lax.axis_size("fsdp")
    dp, fsdp = lax.axis_index("dp"), lax.axis_index("fsdp")
    chips = dp_count // 2
    chip, core = dp // 2, dp % 2
    width = rank // PARTS

    partner = functools.partial(lax.bitwise_xor, fsdp)
    order = jnp.stack([partner(jnp.int32(offset)) for offset in range(fsdp_count)]).astype(jnp.int32)
    hops = jnp.arange(chips, dtype=jnp.int32)
    ring_order = (chip - 1 - hops + chips) % chips
    own_owners = (ring_order * 2 + core).astype(jnp.int32)
    other_owners = (ring_order * 2 + 1 - core).astype(jnp.int32)

    def across(value, offset):
        return lax.ppermute(value, "fsdp", [(index, index ^ offset) for index in range(fsdp_count)])

    def sibling(value):
        return lax.ppermute(value, "dp", [(index, index ^ 1) for index in range(dp_count)])

    def onward(value):
        return lax.ppermute(value, "dp", [(index, (index + 2) % dp_count) for index in range(dp_count)])

    partials = [project(features, basis, order, part, width) for part in range(PARTS)]
    grads_t = out_grads[0].reshape(tokens, dp_count, owned).transpose(1, 2, 0)

    held = ()
    directions = []
    for part in range(PARTS):
        pieces = partials[part]
        mine = total_of([pieces[0]] + [across(pieces[offset], offset) for offset in range(1, fsdp_count)])
        projected = [mine] + [across(mine, offset) for offset in range(1, fsdp_count)]
        other = sibling(gradient(grads_t, projected, order, other_owners))
        own = gradient(grads_t, projected, order, own_owners)
        travelling = onward(total_of([own[0], other[0]]))
        for hop in range(1, chips - 1):
            travelling = onward(total_of([travelling, own[hop], other[hop]]))
        first_next, second_next, direction = adam(
            travelling, own, other, first_moment[0], second_moment[0], held, part
        )
        held = (first_next, second_next)
        directions.append([direction] + [across(direction, offset) for offset in range(1, fsdp_count)])

    update = ()
    for offset in range(fsdp_count):
        update = (
            expand(
                [gathered[offset] for gathered in directions],
                basis,
                order[offset : offset + 1],
                update,
                fsdp_count,
            ),
        )
    return (update[0][None], held[0][None], held[1][None])


def solution(mesh):
    in_specs = (
        P(None, "dp", "fsdp"),
        P(None, "dp", "fsdp"),
        P(None, "fsdp", None),
        P(None, ("fsdp", "dp"), None),
        P(None, ("fsdp", "dp"), None),
    )
    out_specs = (
        P(None, None, "dp", "fsdp"),
        P(None, ("fsdp", "dp"), None),
        P(None, ("fsdp", "dp"), None),
    )
    return jax.shard_map(local, mesh=mesh, in_specs=in_specs, out_specs=out_specs, check_vma=False)
```

```python
import functools

import jax
import jax.numpy as jnp
from jax import lax
from jax.experimental import pallas as pl
from jax.experimental.pallas import tpu as pltpu
from jax.sharding import PartitionSpec as P

beta_first = 0.9
beta_second = 0.999
adam_count = 100.0
epsilon = 1e-08

F32 = jnp.float32
BF16 = jnp.bfloat16
VMEM_LIMIT = 56 * 1024 * 1024
PARTS = 4


def adam(place, arrived, own, other, first, second, held, part):
    owned, rank = first.shape
    width = arrived.shape[1]
    block = min(128, width)
    steps = width // block

    def kernel(place_ref, arrived_ref, own_ref, other_ref, first_ref, second_ref, *refs):
        first_out, second_out, direction_out = refs[-3:]
        grad_low = arrived_ref[...].astype(F32) + own_ref[0].astype(F32) + other_ref[0].astype(F32)
        first_next = beta_first * first_ref[...] + (1.0 - beta_first) * grad_low
        second_next = beta_second * second_ref[...] + (1.0 - beta_second) * grad_low * grad_low
        first_out[...] = first_next
        second_out[...] = second_next
        bias_first = 1.0 - beta_first**adam_count
        bias_second = 1.0 - beta_second**adam_count
        direction = first_next / bias_first / (jnp.sqrt(second_next / bias_second) + epsilon)
        direction_out[...] = direction.astype(BF16)

    column = pl.BlockSpec((owned, block), lambda i, place_ref: (0, part * steps + i))
    narrow = pl.BlockSpec((owned, block), lambda i, place_ref: (0, i))
    return pl.pallas_call(
        kernel,
        out_shape=[
            jax.ShapeDtypeStruct((owned, rank), F32),
            jax.ShapeDtypeStruct((owned, rank), F32),
            jax.ShapeDtypeStruct((owned, width), BF16),
        ],
        grid_spec=pltpu.PrefetchScalarGridSpec(
            num_scalar_prefetch=1,
            grid=(steps,),
            in_specs=[
                narrow,
                pl.BlockSpec((1, owned, block), lambda i, place_ref: (place_ref[0], 0, i)),
                pl.BlockSpec((1, owned, block), lambda i, place_ref: (place_ref[0], 0, i)),
                column,
                column,
            ]
            + [pl.BlockSpec(memory_space=pl.ANY)] * len(held),
            out_specs=[column, column, narrow],
        ),
        input_output_aliases={6 + index: index for index in range(len(held))},
        compiler_params=pltpu.CompilerParams(vmem_limit_bytes=VMEM_LIMIT),
        cost_estimate=pl.CostEstimate(
            flops=12 * owned * width, bytes_accessed=24 * owned * width, transcendentals=owned * width
        ),
        name="adam",
    )(place, arrived, own, other, first, second, *held)


def expand(target, gathered, last, basis_t, held):
    owned, width = last.shape
    rank, features = basis_t.shape
    count = gathered[0].shape[0]
    block = min(512, features)

    def kernel(target_ref, basis_ref, last_ref, *refs):
        gathered_refs, out_ref, whole_ref = refs[: len(gathered)], refs[-2], refs[-1]

        @pl.when(pl.program_id(0) == 0)
        def _():
            for index, gathered_ref in enumerate(gathered_refs):
                whole_ref[:, index * width : (index + 1) * width] = gathered_ref[0]
            whole_ref[:, rank - width :] = last_ref[...]

        out_ref[0] = jnp.dot(whole_ref[...], basis_ref[...], preferred_element_type=F32)

    return pl.pallas_call(
        kernel,
        out_shape=jax.ShapeDtypeStruct((count, owned, features), F32),
        grid_spec=pltpu.PrefetchScalarGridSpec(
            num_scalar_prefetch=1,
            grid=(features // block,),
            in_specs=[
                pl.BlockSpec((rank, block), lambda i, target_ref: (0, i)),
                pl.BlockSpec((owned, width), lambda i, target_ref: (0, 0)),
            ]
            + [pl.BlockSpec((1, owned, width), lambda i, target_ref: (target_ref[0], 0, 0))] * len(gathered)
            + [pl.BlockSpec(memory_space=pl.ANY)] * len(held),
            out_specs=pl.BlockSpec((1, owned, block), lambda i, target_ref: (target_ref[0], 0, i)),
            scratch_shapes=[pltpu.VMEM((owned, rank), BF16)],
        ),
        input_output_aliases={3 + len(gathered): 0} if held else {},
        compiler_params=pltpu.CompilerParams(vmem_limit_bytes=VMEM_LIMIT),
        cost_estimate=pl.CostEstimate(
            flops=2 * owned * rank * features,
            bytes_accessed=2 * (owned * rank + rank * features) + 4 * owned * features,
            transcendentals=0,
        ),
        name="expand",
    )(target, basis_t, last, *gathered, *held)


def transpose(value):
    rows, columns = value.shape
    block = min(512, rows)

    def kernel(value_ref, out_ref):
        out_ref[...] = value_ref[...].T

    return pl.pallas_call(
        kernel,
        out_shape=jax.ShapeDtypeStruct((columns, rows), value.dtype),
        grid=(rows // block,),
        in_specs=[pl.BlockSpec((block, columns), lambda i: (i, 0))],
        out_specs=pl.BlockSpec((columns, block), lambda i: (0, i)),
        compiler_params=pltpu.CompilerParams(vmem_limit_bytes=VMEM_LIMIT),
        cost_estimate=pl.CostEstimate(flops=0, bytes_accessed=4 * rows * columns, transcendentals=0),
        name="transpose",
    )(value)


def total_of(*terms):
    total = terms[0].astype(F32)
    for term in terms[1:]:
        total = total + term.astype(F32)
    return total.astype(BF16)


def after(value, *earlier):
    return lax.optimization_barrier((value, *earlier))[0]


def local(activations, out_grads, projector, first_moment, second_moment):
    owned = first_moment.shape[1]
    features = activations[0]
    basis = projector[0]
    rank = basis.shape[1]
    tokens = features.shape[0]
    dp_count, fsdp_count = lax.axis_size("dp"), lax.axis_size("fsdp")
    dp, fsdp = lax.axis_index("dp"), lax.axis_index("fsdp")
    chips = dp_count // 2
    chip, core = dp // 2, dp % 2
    width = rank // PARTS

    offsets = [1 << bit for bit in range(fsdp_count.bit_length() - 1)]
    order = jnp.stack([fsdp ^ offset for offset in range(fsdp_count)]).astype(jnp.int32)
    place = jnp.stack([chip, core]).astype(jnp.int32)

    def across(value, offset):
        return lax.ppermute(value, "fsdp", [(index, index ^ offset) for index in range(fsdp_count)])

    def sibling(value):
        return lax.ppermute(value, "dp", [(index, index ^ 1) for index in range(dp_count)])

    def onward(value):
        return lax.ppermute(value, "dp", [(index, (index + 2) % dp_count) for index in range(dp_count)])

    def sum_step(halves, step):
        return [
            total_of(half, across(half, steps[step])) for half, steps in zip(halves, (offsets, offsets[::-1]))
        ]

    def halves_of(value):
        return [value[: tokens // 2], value[tokens // 2 :]]

    def gradient(projected):
        product = lax.dot_general(
            out_grads[0], projected, (((0,), (0,)), ((), ())), preferred_element_type=F32
        ).astype(BF16)
        return product.reshape(chips, 2, owned, projected.shape[1])

    def parity(product, which):
        return lax.dynamic_slice_in_dim(product, which, 1, axis=1)[:, 0]

    def block_at(hop, blocks):
        return lax.dynamic_index_in_dim(blocks, (chip - 1 - hop + chips) % chips, axis=0, keepdims=False)

    early = jnp.dot(features, basis[:, :width], preferred_element_type=F32).astype(BF16)
    late = jnp.dot(after(features, early), basis[:, width:], preferred_element_type=F32).astype(BF16)
    rest = lax.psum(late[:, width:], "fsdp")
    sums_0 = sum_step(halves_of(early), 0)
    basis_t = transpose(after(basis, *sums_0))
    sums_1 = sum_step([after(half, *sums_0) for half in halves_of(late[:, :width])], 0)
    for step in range(1, len(offsets)):
        sums_0 = sum_step(sums_0, step)

    def send_out(product, token):
        outgoing = parity(after(product, token), 1 - core)
        return (parity(product, core), sibling(outgoing)), outgoing

    blocks = [None] * PARTS
    product = gradient(jnp.concatenate(sums_0))
    blocks[0], token = send_out(product, product)
    travelling = [None] * PARTS

    held = ()
    gathered = []
    hops = chips - 1
    for slot in range(hops + PARTS):
        if slot == 1:
            for step in range(1, len(offsets)):
                sums_1 = sum_step(sums_1, step)
            product = gradient(after(jnp.concatenate(sums_1), token))
            blocks[1], token = send_out(product, product)
        if slot == 2:
            product = gradient(after(rest, token))
            for part in range(2, PARTS):
                begin = (part - 2) * width
                blocks[part], token = send_out(product[..., begin : begin + width], token if part > 2 else product)
        for part in range(PARTS):
            hop = slot - part
            if not 0 <= hop <= hops:
                continue
            own, other = blocks[part]
            if hop < hops:
                terms = (block_at(hop, own), block_at(hop, other))
                if hop == 0:
                    leaving = total_of(after(terms[0], token), terms[1])
                else:
                    leaving = total_of(after(travelling[part], token), *terms)
                travelling[part] = onward(leaving)
                token = leaving
            else:
                first_next, second_next, direction = adam(
                    place, after(travelling[part], token), own, other, first_moment[0], second_moment[0], held, part
                )
                held = (first_next, second_next)
                token = direction
                if part < PARTS - 1:
                    if gathered:
                        direction = after(direction, gathered[-1])
                    gathered.append(lax.all_gather(direction, "fsdp"))

    last = [direction] + [across(direction, offset) for offset in range(1, fsdp_count)]
    update = ()
    for offset in range(fsdp_count):
        update = (expand(order[offset : offset + 1], gathered, last[offset], basis_t, update),)
    return (update[0][None], held[0][None], held[1][None])


def solution(mesh):
    in_specs = (
        P(None, "dp", "fsdp"),
        P(None, "dp", "fsdp"),
        P(None, "fsdp", None),
        P(None, ("fsdp", "dp"), None),
        P(None, ("fsdp", "dp"), None),
    )
    out_specs = (
        P(None, None, "dp", "fsdp"),
        P(None, ("fsdp", "dp"), None),
        P(None, ("fsdp", "dp"), None),
    )
    return jax.shard_map(local, mesh=mesh, in_specs=in_specs, out_specs=out_specs, check_vma=False)
```

```python
import functools

import jax
import jax.numpy as jnp
from jax import lax
from jax.experimental import pallas as pl
from jax.experimental.pallas import tpu as pltpu
from jax.sharding import PartitionSpec as P

beta_first = 0.9
beta_second = 0.999
adam_count = 100.0
epsilon = 1e-08

F32 = jnp.float32
BF16 = jnp.bfloat16
VMEM_LIMIT = 56 * 1024 * 1024
COST = pl.CostEstimate(flops=1024, bytes_accessed=1024, transcendentals=0)
PARAMS = pltpu.CompilerParams(vmem_limit_bytes=VMEM_LIMIT)


def transpose(value, block):
    rows, columns = value.shape

    def kernel(value_ref, out_ref):
        out_ref[...] = value_ref[...].T

    return pl.pallas_call(
        kernel,
        out_shape=jax.ShapeDtypeStruct((columns, rows), value.dtype),
        grid=(rows // block,),
        in_specs=[pl.BlockSpec((block, columns), lambda i: (i, 0))],
        out_specs=pl.BlockSpec((columns, block), lambda i: (0, i)),
        compiler_params=PARAMS,
        cost_estimate=COST,
        name="transpose",
    )(value)


def project(features, basis, begin, width):
    tokens, depth = features.shape
    rows = tokens // 4
    blocks = basis.shape[1] // begin

    def kernel(features_ref, *refs):
        basis_refs, (low_ref, high_ref) = refs[:-2], refs[-2:]
        for index, basis_ref in enumerate(basis_refs):
            value = jnp.dot(features_ref[...], basis_ref[...], preferred_element_type=F32).astype(BF16)
            columns = slice(index * begin, (index + 1) * begin)

            @pl.when(pl.program_id(0) < 2)
            def _():
                low_ref[:, columns] = value

            @pl.when(pl.program_id(0) >= 2)
            def _():
                high_ref[:, columns] = value

    return pl.pallas_call(
        kernel,
        out_shape=[jax.ShapeDtypeStruct((tokens // 2, width), BF16)] * 2,
        grid=(4,),
        in_specs=[pl.BlockSpec((rows, depth), lambda i: (i, 0))]
        + [pl.BlockSpec((depth, begin), functools.partial(lambda at, i: (0, at), at)) for at in range(1, blocks)],
        out_specs=[
            pl.BlockSpec((rows, width), lambda i: (jnp.minimum(i, 1), 0)),
            pl.BlockSpec((rows, width), lambda i: (jnp.maximum(i - 2, 0), 0)),
        ],
        compiler_params=PARAMS,
        cost_estimate=COST,
        name="project",
    )(features, *[basis] * (blocks - 1))


def gradient(grads_t, halves, owners, widths):
    _, owned, tokens = grads_t.shape
    rows, width = halves[0].shape
    count = owners.shape[0]

    def kernel(owners_ref, grads_ref, low_ref, high_ref, *refs):
        out_refs, whole_ref = refs[:-1], refs[-1]

        @pl.when(pl.program_id(0) == 0)
        def _():
            whole_ref[:rows, :] = low_ref[...]
            whole_ref[rows:, :] = high_ref[...]

        value = jnp.dot(grads_ref[0], whole_ref[...], preferred_element_type=F32).astype(BF16)
        begin = 0
        for out_ref, size in zip(out_refs, widths):
            out_ref[0] = value[:, begin : begin + size]
            begin += size

    return pl.pallas_call(
        kernel,
        out_shape=[jax.ShapeDtypeStruct((count, owned, size), BF16) for size in widths],
        grid_spec=pltpu.PrefetchScalarGridSpec(
            num_scalar_prefetch=1,
            grid=(count,),
            in_specs=[pl.BlockSpec((1, owned, tokens), lambda i, owners_ref: (owners_ref[i], 0, 0))]
            + [pl.BlockSpec((rows, width), lambda i, owners_ref: (0, 0))] * 2,
            out_specs=[pl.BlockSpec((1, owned, size), lambda i, owners_ref: (i, 0, 0)) for size in widths],
            scratch_shapes=[pltpu.VMEM((tokens, width), BF16)],
        ),
        compiler_params=PARAMS,
        cost_estimate=COST,
        name="gradient",
    )(owners, grads_t, *halves)


def accumulate(arrived, own, coming, hop):
    _, owned, width = own.shape

    def kernel(*refs):
        out_ref = refs[-1]
        total = refs[0][0].astype(F32) + refs[1][0].astype(F32)
        if arrived:
            total = total + refs[2][...].astype(F32)
        out_ref[...] = total.astype(BF16)

    block = pl.BlockSpec((1, owned, width), lambda i: (hop, 0, 0))
    return pl.pallas_call(
        kernel,
        grid=(1,),
        out_shape=jax.ShapeDtypeStruct((owned, width), BF16),
        in_specs=[block, block] + [pl.BlockSpec(memory_space=pltpu.VMEM)] * len(arrived),
        out_specs=pl.BlockSpec(memory_space=pltpu.VMEM),
        compiler_params=PARAMS,
        cost_estimate=COST,
        name="accumulate",
    )(own, coming, *arrived)


def adam(pieces, first, second, held, begin):
    owned, rank = first.shape
    widths = [piece[0].shape[1] for piece in pieces]
    width = sum(widths)
    last = pieces[0][1].shape[0] - 1

    def kernel(*refs):
        first_ref, second_ref = refs[3 * len(pieces) : 3 * len(pieces) + 2]
        first_out, second_out, direction_out = refs[-3:]
        at = 0
        for index, size in enumerate(widths):
            arrived_ref, own_ref, other_ref = refs[3 * index : 3 * index + 3]
            columns = slice(at, at + size)
            at += size
            grad_low = arrived_ref[...].astype(F32) + own_ref[0].astype(F32) + other_ref[0].astype(F32)
            first_next = beta_first * first_ref[:, columns] + (1.0 - beta_first) * grad_low
            second_next = beta_second * second_ref[:, columns] + (1.0 - beta_second) * grad_low * grad_low
            first_out[:, columns] = first_next
            second_out[:, columns] = second_next
            bias_first = 1.0 - beta_first**adam_count
            bias_second = 1.0 - beta_second**adam_count
            direction = first_next / bias_first / (jnp.sqrt(second_next / bias_second) + epsilon)
            direction_out[:, columns] = direction.astype(BF16)

    column = pl.BlockSpec((owned, width), lambda i: (0, begin // width))
    piece_specs = []
    for size in widths:
        piece_specs += [pl.BlockSpec(memory_space=pltpu.VMEM)]
        piece_specs += [pl.BlockSpec((1, owned, size), lambda i: (last, 0, 0))] * 2
    inputs = len(piece_specs) + 2
    return pl.pallas_call(
        kernel,
        grid=(1,),
        out_shape=[
            jax.ShapeDtypeStruct((owned, rank), F32),
            jax.ShapeDtypeStruct((owned, rank), F32),
            jax.ShapeDtypeStruct((owned, width), BF16),
        ],
        in_specs=piece_specs + [column, column] + [pl.BlockSpec(memory_space=pl.ANY)] * len(held),
        out_specs=[column, column, pl.BlockSpec((owned, width), lambda i: (0, 0))],
        input_output_aliases={inputs + index: index for index in range(len(held))},
        compiler_params=PARAMS,
        cost_estimate=COST,
        name="adam",
    )(*[array for piece in pieces for array in piece], first, second, *held)


def expand(target, directions, basis_t, held, count):
    owned, width = directions[0].shape
    rank, features = basis_t.shape
    block = min(1024, features)

    def kernel(target_ref, basis_ref, *refs):
        direction_refs, out_ref, whole_ref = refs[: len(directions)], refs[-2], refs[-1]

        @pl.when(pl.program_id(0) == 0)
        def _():
            for index, direction_ref in enumerate(direction_refs):
                whole_ref[:, index * width : (index + 1) * width] = direction_ref[...]

        out_ref[0] = jnp.dot(whole_ref[...], basis_ref[...], preferred_element_type=F32)

    return pl.pallas_call(
        kernel,
        out_shape=jax.ShapeDtypeStruct((count, owned, features), F32),
        grid_spec=pltpu.PrefetchScalarGridSpec(
            num_scalar_prefetch=1,
            grid=(features // block,),
            in_specs=[pl.BlockSpec((rank, block), lambda i, target_ref: (0, i))]
            + [pl.BlockSpec((owned, width), lambda i, target_ref: (0, 0))] * len(directions)
            + [pl.BlockSpec(memory_space=pl.ANY)] * len(held),
            out_specs=pl.BlockSpec((1, owned, block), lambda i, target_ref: (target_ref[0], 0, i)),
            scratch_shapes=[pltpu.VMEM((owned, rank), BF16)],
        ),
        input_output_aliases={2 + len(directions): 0} if held else {},
        compiler_params=PARAMS,
        cost_estimate=COST,
        name="expand",
    )(target, basis_t, *directions, *held)


def total_of(*terms):
    total = terms[0].astype(F32)
    for term in terms[1:]:
        total = total + term.astype(F32)
    return total.astype(BF16)


def after(value, *earlier):
    return lax.optimization_barrier((value, *earlier))[0]


def local(activations, out_grads, projector, first_moment, second_moment):
    owned = first_moment.shape[1]
    features = activations[0]
    basis = projector[0]
    rank = basis.shape[1]
    tokens = features.shape[0]
    dp_count, fsdp_count = lax.axis_size("dp"), lax.axis_size("fsdp")
    dp, fsdp = lax.axis_index("dp"), lax.axis_index("fsdp")
    chips = dp_count // 2
    chip, core = dp // 2, dp % 2
    width = rank // 4

    offsets = [1 << bit for bit in range(fsdp_count.bit_length() - 1)]
    order = jnp.stack([fsdp ^ offset for offset in range(fsdp_count)]).astype(jnp.int32)
    hops = chips - 1
    ring_order = (chip - 1 - jnp.arange(chips, dtype=jnp.int32) + chips) % chips
    own_owners = (ring_order * 2 + core).astype(jnp.int32)
    other_owners = (ring_order * 2 + 1 - core).astype(jnp.int32)

    def across(value, offset):
        return lax.ppermute(value, "fsdp", [(index, index ^ offset) for index in range(fsdp_count)])

    def sibling(value):
        return lax.ppermute(value, "dp", [(index, index ^ 1) for index in range(dp_count)])

    def onward(value):
        return lax.ppermute(value, "dp", [(index, (index + 2) % dp_count) for index in range(dp_count)])

    def exchange(halves, step):
        return [across(half, steps[step]) for half, steps in zip(halves, (offsets, offsets[::-1]))]

    def add(halves, arrived):
        return [total_of(half, term) for half, term in zip(halves, arrived)]

    early = jnp.dot(features, basis[:, :width], preferred_element_type=F32).astype(BF16)
    sums_0 = [early[: tokens // 2], early[tokens // 2 :]]
    coming_0 = exchange(sums_0, 0)
    sums_1 = project(after(features, early), basis, width, rank - width)
    sums_0 = add(sums_0, [after(term, *sums_1) for term in coming_0])
    for step in range(1, len(offsets) - 1):
        sums_0 = add(sums_0, exchange(sums_0, step))
    coming_0 = exchange(sums_0, len(offsets) - 1)
    sums_1 = [after(half, *sums_0) for half in sums_1]
    coming_1 = exchange(sums_1, 0)
    grads_t = transpose(after(out_grads[0], *sums_0), min(256, tokens)).reshape(dp_count, owned, tokens)
    sums_0 = add(sums_0, [after(term, grads_t) for term in coming_0])

    def blocks_of(grads_t, sums, widths, between=lambda token: []):
        other = gradient(grads_t, sums, other_owners, widths)
        coming = [sibling(value) for value in other]
        own = gradient(after(grads_t, *other, *between(other[0])), sums, own_owners, widths)
        return own, coming

    def ring(parts, stride, token, between, finish):
        events = sorted(
            (2 * hop + stride * part, part, hop) for part in range(len(parts)) for hop in range(hops + 1)
        )
        arrived = [None] * len(parts)
        for number, (_, part, hop) in enumerate(events):
            own, coming = parts[part]
            if hop < hops:
                before = () if arrived[part] is None else (arrived[part],)
                token = accumulate(before, after(own, token), coming, hop)
                arrived[part] = onward(token)
            else:
                token = finish(part, after(arrived[part], token), token)
            if number in between:
                token = between[number](token, arrived)
        return token

    held = ()
    directions = []

    def step_of(pieces, begin):
        nonlocal held
        first_next, second_next, direction = adam(pieces, first_moment[0], second_moment[0], held, begin)
        held = (first_next, second_next)
        directions.append([direction] + [across(direction, offset) for offset in range(1, fsdp_count)])
        return direction

    rest = {}
    waiting = []

    def middle(token):
        sums = add(sums_1, [after(term, token) for term in coming_1])
        for step in range(1, len(offsets)):
            coming = exchange(sums, step)
            if step == len(offsets) - 1:
                rest["sums"], rest["coming"] = sums, coming
            else:
                sums = add(sums, coming)
        return sums

    own, coming = blocks_of(grads_t, sums_0, [width // 2] * 2, middle)
    parts_0 = list(zip(own, coming))

    def finish_0(part, arrived, token):
        waiting.append((arrived, *parts_0[part]))
        return step_of(waiting, 0) if len(waiting) == len(parts_0) else token

    def last(token, arrived):
        basis_t = transpose(after(basis, token), min(512, basis.shape[0]))
        sums = add(rest["sums"], [after(term, basis_t, *arrived) for term in rest["coming"]])
        rest["basis_t"] = basis_t
        own, coming = blocks_of(grads_t, sums, [width] * 3)
        rest["parts"] = list(zip(own, coming))
        return own[0]

    final_send = 2 * hops - 1
    token = ring(parts_0, 1, own[0], {final_send: last}, finish_0)
    parts_1 = rest["parts"]

    def finish_1(part, arrived, token):
        if part in (0, 2):
            arrived = after(arrived, *directions[part // 2])
        return step_of([(arrived, *parts_1[part])], (part + 1) * width)

    ring(parts_1, 1.5, token, {}, finish_1)

    directions[-1][0] = after(directions[-1][0], *directions[-2])
    update = ()
    for offset in range(fsdp_count):
        update = (
            expand(
                order[offset : offset + 1],
                [gathered[offset] for gathered in directions],
                rest["basis_t"],
                update,
                fsdp_count,
            ),
        )
    return (update[0][None], held[0][None], held[1][None])


def solution(mesh):
    in_specs = (
        P(None, "dp", "fsdp"),
        P(None, "dp", "fsdp"),
        P(None, "fsdp", None),
        P(None, ("fsdp", "dp"), None),
        P(None, ("fsdp", "dp"), None),
    )
    out_specs = (
        P(None, None, "dp", "fsdp"),
        P(None, ("fsdp", "dp"), None),
        P(None, ("fsdp", "dp"), None),
    )
    return jax.shard_map(local, mesh=mesh, in_specs=in_specs, out_specs=out_specs, check_vma=False)
```

```python
import functools

import jax
import jax.numpy as jnp
from jax import lax
from jax.experimental import pallas as pl
from jax.experimental.pallas import tpu as pltpu
from jax.sharding import PartitionSpec as P

beta_first = 0.9
beta_second = 0.999
adam_count = 100.0
epsilon = 1e-08

F32 = jnp.float32
BF16 = jnp.bfloat16
VMEM_LIMIT = 64 * 1024 * 1024
COST = pl.CostEstimate(flops=1024, bytes_accessed=1024, transcendentals=0)
PARAMS = pltpu.CompilerParams(vmem_limit_bytes=VMEM_LIMIT)


def transpose(value, block, begin=0, count=None, held=()):
    rows, columns = value.shape
    count = rows // block if count is None else count

    def kernel(value_ref, *refs):
        refs[-1][...] = value_ref[...].T

    return pl.pallas_call(
        kernel,
        out_shape=jax.ShapeDtypeStruct((columns, rows), value.dtype),
        grid=(count,),
        in_specs=[pl.BlockSpec((block, columns), lambda i: (begin + i, 0))]
        + [pl.BlockSpec(memory_space=pl.ANY)] * len(held),
        out_specs=pl.BlockSpec((columns, block), lambda i: (0, begin + i)),
        input_output_aliases={1: 0} if held else {},
        compiler_params=PARAMS,
        cost_estimate=COST,
        name="transpose",
    )(value, *held)


def gradient(grads_t, halves, owners, widths, arrived=()):
    _, owned, tokens = grads_t.shape
    rows, width = halves[0].shape
    count = owners.shape[0]
    top = (owned // 2 + 15) // 16 * 16

    def kernel(owners_ref, grads_ref, low_ref, high_ref, *refs):
        arrived_refs, out_refs, whole_ref = refs[: len(arrived)], refs[len(arrived) : -1], refs[-1]

        @pl.when(pl.program_id(0) == 0)
        def _():
            whole_ref[:rows, :] = low_ref[...]
            whole_ref[rows:, :] = high_ref[...]

        for part in (slice(0, top), slice(top, owned)):
            value = jnp.dot(grads_ref[0, part, :], whole_ref[...], preferred_element_type=F32)
            begin = 0
            for run, size in enumerate(widths):
                columns = value[:, begin : begin + size]
                begin += size
                if not arrived:
                    out_refs[run][0, part, :] = columns.astype(BF16)
                    continue
                columns = (columns + arrived_refs[run][0, part, :].astype(F32)).astype(BF16)
                for block in range(count):

                    @pl.when(pl.program_id(0) == block)
                    def _(out_ref=out_refs[run * count + block], columns=columns):
                        out_ref[part, :] = columns

    if arrived:
        out_shape = [jax.ShapeDtypeStruct((owned, size), BF16) for size in widths for _ in range(count)]
        out_specs = [pl.BlockSpec(out.shape, lambda i, owners_ref: (0, 0)) for out in out_shape]
    else:
        out_shape = [jax.ShapeDtypeStruct((count, owned, size), BF16) for size in widths]
        out_specs = [pl.BlockSpec((1, owned, size), lambda i, owners_ref: (i, 0, 0)) for size in widths]
    results = pl.pallas_call(
        kernel,
        out_shape=out_shape,
        grid_spec=pltpu.PrefetchScalarGridSpec(
            num_scalar_prefetch=1,
            grid=(count,),
            in_specs=[pl.BlockSpec((1, owned, tokens), lambda i, owners_ref: (owners_ref[i], 0, 0))]
            + [pl.BlockSpec((rows, width), lambda i, owners_ref: (0, 0))] * 2
            + [pl.BlockSpec((1, owned, term.shape[2]), lambda i, owners_ref: (i, 0, 0)) for term in arrived],
            out_specs=out_specs,
            scratch_shapes=[pltpu.VMEM((tokens, width), BF16)],
        ),
        compiler_params=PARAMS,
        cost_estimate=COST,
        name="gradient",
    )(owners, grads_t, *halves, *arrived)
    return [results[run * count : (run + 1) * count] for run in range(len(widths))] if arrived else results


def accumulate(arrived, own):
    def kernel(arrived_ref, own_ref, out_ref):
        out_ref[...] = (arrived_ref[...].astype(F32) + own_ref[...].astype(F32)).astype(BF16)

    return pl.pallas_call(
        kernel,
        out_shape=jax.ShapeDtypeStruct(own.shape, BF16),
        in_specs=[pl.BlockSpec(memory_space=pltpu.VMEM)] * 2,
        out_specs=pl.BlockSpec(memory_space=pltpu.VMEM),
        compiler_params=PARAMS,
        cost_estimate=COST,
        name="accumulate",
    )(arrived, own)


def adam(pieces, first, second, held, begin):
    owned, rank = first.shape
    widths = [piece[0].shape[1] for piece in pieces]
    width = sum(widths)

    def kernel(*refs):
        first_ref, second_ref = refs[2 * len(pieces) : 2 * len(pieces) + 2]
        first_out, second_out, direction_out = refs[-3:]
        at = 0
        for index, size in enumerate(widths):
            arrived_ref, own_ref = refs[2 * index : 2 * index + 2]
            columns = slice(at, at + size)
            at += size
            grad_low = arrived_ref[...].astype(F32) + own_ref[...].astype(F32)
            first_next = beta_first * first_ref[:, columns] + (1.0 - beta_first) * grad_low
            second_next = beta_second * second_ref[:, columns] + (1.0 - beta_second) * grad_low * grad_low
            first_out[:, columns] = first_next
            second_out[:, columns] = second_next
            bias_first = 1.0 - beta_first**adam_count
            bias_second = 1.0 - beta_second**adam_count
            direction = first_next / bias_first / (jnp.sqrt(second_next / bias_second) + epsilon)
            direction_out[:, columns] = direction.astype(BF16)

    column = pl.BlockSpec((owned, width), lambda i: (0, begin // width))
    piece_specs = [pl.BlockSpec(memory_space=pltpu.VMEM)] * (2 * len(pieces))
    inputs = len(piece_specs) + 2
    return pl.pallas_call(
        kernel,
        grid=(1,),
        out_shape=[
            jax.ShapeDtypeStruct((owned, rank), F32),
            jax.ShapeDtypeStruct((owned, rank), F32),
            jax.ShapeDtypeStruct((owned, width), BF16),
        ],
        in_specs=piece_specs + [column, column] + [pl.BlockSpec(memory_space=pl.ANY)] * len(held),
        out_specs=[column, column, pl.BlockSpec((owned, width), lambda i: (0, 0))],
        input_output_aliases={inputs + index: index for index in range(len(held))},
        compiler_params=PARAMS,
        cost_estimate=COST,
        name="adam",
    )(*[array for piece in pieces for array in piece], first, second, *held)


def expand(target, directions, basis_t, held, count):
    owned, width = directions[0].shape
    rank, features = basis_t.shape
    block = min(1024, features)

    def kernel(target_ref, basis_ref, *refs):
        direction_refs, out_ref, whole_ref = refs[: len(directions)], refs[-2], refs[-1]

        @pl.when(pl.program_id(0) == 0)
        def _():
            for index, direction_ref in enumerate(direction_refs):
                whole_ref[:, index * width : (index + 1) * width] = direction_ref[...]

        out_ref[0] = jnp.dot(whole_ref[...], basis_ref[...], preferred_element_type=F32)

    return pl.pallas_call(
        kernel,
        out_shape=jax.ShapeDtypeStruct((count, owned, features), F32),
        grid_spec=pltpu.PrefetchScalarGridSpec(
            num_scalar_prefetch=1,
            grid=(features // block,),
            in_specs=[pl.BlockSpec((rank, block), lambda i, target_ref: (0, i))]
            + [pl.BlockSpec((owned, width), lambda i, target_ref: (0, 0))] * len(directions)
            + [pl.BlockSpec(memory_space=pl.ANY)] * len(held),
            out_specs=pl.BlockSpec((1, owned, block), lambda i, target_ref: (target_ref[0], 0, i)),
            scratch_shapes=[pltpu.VMEM((owned, rank), BF16)],
        ),
        input_output_aliases={2 + len(directions): 0} if held else {},
        compiler_params=PARAMS,
        cost_estimate=COST,
        name="expand",
    )(target, basis_t, *directions, *held)


def total_of(*terms):
    total = terms[0].astype(F32)
    for term in terms[1:]:
        total = total + term.astype(F32)
    return total.astype(BF16)


def after(value, *earlier):
    return lax.optimization_barrier((value, *earlier))[0]


def local(activations, out_grads, projector, first_moment, second_moment):
    owned = first_moment.shape[1]
    features = activations[0]
    basis = projector[0]
    rank = basis.shape[1]
    tokens = features.shape[0]
    dp_count, fsdp_count = lax.axis_size("dp"), lax.axis_size("fsdp")
    dp, fsdp = lax.axis_index("dp"), lax.axis_index("fsdp")
    chips = dp_count // 2
    chip, core = dp // 2, dp % 2
    width = rank // 4

    offsets = [1 << bit for bit in range(fsdp_count.bit_length() - 1)]
    order = jnp.stack([fsdp ^ offset for offset in range(fsdp_count)]).astype(jnp.int32)
    hops = chips - 1
    ring_order = (chip - 1 - jnp.arange(chips, dtype=jnp.int32) + chips) % chips
    own_owners = (ring_order * 2 + core).astype(jnp.int32)
    other_owners = (ring_order * 2 + 1 - core).astype(jnp.int32)

    def across(value, offset):
        return lax.ppermute(value, "fsdp", [(index, index ^ offset) for index in range(fsdp_count)])

    def sibling(value):
        return lax.ppermute(value, "dp", [(index, index ^ 1) for index in range(dp_count)])

    def onward(value):
        return lax.ppermute(value, "dp", [(index, (index + 2) % dp_count) for index in range(dp_count)])

    def exchange(halves, step):
        return [across(half, steps[step]) for half, steps in zip(halves, (offsets, offsets[::-1]))]

    def add(halves, arrived):
        return [total_of(half, term) for half, term in zip(halves, arrived)]

    partial = jnp.dot(features, basis, preferred_element_type=F32).astype(BF16)
    low, high = partial[: tokens // 2], partial[tokens // 2 :]
    sums_0 = [low[:, :width], high[:, :width]]
    sums_1 = [low[:, width:], high[:, width:]]
    coming_0 = exchange(sums_0, 0)
    block = tokens // 4
    grads_t = transpose(after(out_grads[0], *sums_0), block, 0, 2)
    sums_0 = add(sums_0, [after(term, grads_t) for term in coming_0])
    for step in range(1, len(offsets) - 1):
        sums_0 = add(sums_0, exchange(sums_0, step))
    coming_0 = exchange(sums_0, len(offsets) - 1)
    grads_t = transpose(after(out_grads[0], *sums_0), block, 2, 2, (grads_t,)).reshape(dp_count, owned, tokens)
    coming_1 = exchange([after(half, grads_t) for half in sums_1], 0)
    sums_0 = add(sums_0, [after(term, grads_t) for term in coming_0])
    other = gradient(grads_t, sums_0, other_owners, [width // 2] * 2)
    coming = [sibling(value) for value in other]
    sums_1 = add(sums_1, [after(term, *other) for term in coming_1])
    for step in range(1, len(offsets) - 1):
        sums_1 = add(sums_1, exchange(sums_1, step))
    coming_1 = exchange(sums_1, len(offsets) - 1)
    parts_0 = gradient(after(grads_t, *sums_1), sums_0, own_owners, [width // 2] * 2, coming)

    def ring(parts, stride, token, between, finish):
        events = sorted(
            (2 * hop + stride * part, part, hop)
            for part in range(len(parts))
            for hop in range(hops + (finish is not None))
        )
        arrived = [None] * len(parts)
        for number, (_, part, hop) in enumerate(events):
            if hop == hops:
                token = finish(part, after(arrived[part], token))
            else:
                leaving = parts[part][hop] if hop == 0 else accumulate(arrived[part], after(parts[part][hop], token))
                arrived[part] = onward(leaving)
                token = leaving
            if number in between:
                token = between[number](token, arrived)
        return token, arrived

    held = ()
    directions = []
    rest = {}

    def step_of(pieces, begin, *earlier):
        nonlocal held
        first_next, second_next, direction = adam(pieces, first_moment[0], second_moment[0], held, begin)
        held = (first_next, second_next)
        sent = after(direction, *earlier) if earlier else direction
        directions.append([direction] + [across(sent, offset) for offset in range(1, fsdp_count)])
        return direction

    def send_other(token, arrived):
        rest["sums"] = add(sums_1, [after(term, token) for term in coming_1])
        rest["other"] = gradient(grads_t, rest["sums"], other_owners, [width] * 3)
        return rest["other"][0]

    def start_rest(token, arrived):
        coming = [sibling(after(value, token)) for value in rest["other"]]
        rest["basis_t"] = transpose(after(basis, token), min(512, basis.shape[0]))
        tied = after(grads_t, rest["basis_t"], *arrived)
        rest["parts"] = gradient(tied, rest["sums"], own_owners, [width] * 3, coming)
        return rest["parts"][0][0]

    token, last_0 = ring(
        parts_0, 1, parts_0[0][0], {3: send_other, 2 * hops - 1: start_rest}, None
    )

    def finish_0(token, arrived):
        pieces = [(after(value, token), part[hops]) for value, part in zip(last_0, parts_0)]
        return step_of(pieces, 0)

    def finish_1(part, arrived):
        earlier = directions[part - 1] if part > 0 else ()
        return step_of([(arrived, rest["parts"][part][hops])], (part + 1) * width, *earlier)

    ring(rest["parts"], 1.5, token, {1: finish_0}, finish_1)

    update = ()
    for offset in range(fsdp_count):
        pieces = [gathered[offset] for gathered in directions]
        if offset == 1:
            pieces[-1] = after(pieces[-1], *directions[-2])
        update = (expand(order[offset : offset + 1], pieces, rest["basis_t"], update, fsdp_count),)
    return (update[0][None], held[0][None], held[1][None])


def solution(mesh):
    in_specs = (
        P(None, "dp", "fsdp"),
        P(None, "dp", "fsdp"),
        P(None, "fsdp", None),
        P(None, ("fsdp", "dp"), None),
        P(None, ("fsdp", "dp"), None),
    )
    out_specs = (
        P(None, None, "dp", "fsdp"),
        P(None, ("fsdp", "dp"), None),
        P(None, ("fsdp", "dp"), None),
    )
    return jax.shard_map(local, mesh=mesh, in_specs=in_specs, out_specs=out_specs, check_vma=False)
```

```python
import functools

import jax
import jax.numpy as jnp
from jax import lax
from jax.experimental import pallas as pl
from jax.experimental.pallas import tpu as pltpu
from jax.sharding import PartitionSpec as P

beta_first = 0.9
beta_second = 0.999
adam_count = 100.0
epsilon = 1e-08

F32 = jnp.float32
BF16 = jnp.bfloat16
COST = pl.CostEstimate(flops=1024, bytes_accessed=1 << 20, transcendentals=0)
PARAMS = pltpu.CompilerParams(vmem_limit_bytes=40 * 1024 * 1024)
RING_PARAMS = pltpu.CompilerParams(vmem_limit_bytes=64 * 1024 * 1024)


def transpose(value, block, begin=0, count=None, held=()):
    rows, columns = value.shape
    count = rows // block if count is None else count

    def kernel(value_ref, *refs):
        refs[-1][...] = value_ref[...].T

    return pl.pallas_call(
        kernel,
        out_shape=jax.ShapeDtypeStruct((columns, rows), value.dtype),
        grid=(count,),
        in_specs=[pl.BlockSpec((block, columns), lambda i: (begin + i, 0))]
        + [pl.BlockSpec(memory_space=pl.ANY)] * len(held),
        out_specs=pl.BlockSpec((columns, block), lambda i: (0, begin + i)),
        input_output_aliases={1: 0} if held else {},
        compiler_params=PARAMS,
        cost_estimate=COST,
        name="transpose",
    )(value, *held)


def plus(one, two):
    rows, width = one.shape
    block = pl.BlockSpec((rows // 2, width), lambda i: (i, 0))

    def kernel(one_ref, two_ref, out_ref):
        out_ref[...] = (one_ref[...].astype(F32) + two_ref[...].astype(F32)).astype(BF16)

    return pl.pallas_call(
        kernel,
        grid=(2,),
        out_shape=jax.ShapeDtypeStruct(one.shape, BF16),
        in_specs=[block, block],
        out_specs=block,
        compiler_params=RING_PARAMS,
        cost_estimate=COST,
        name="plus",
    )(one, two)


def gradient(grads_t, pieces, owners, cuts):
    _, owned, tokens = grads_t.shape
    rows, run = pieces[0].shape
    width = run * len(pieces) // 2
    count = owners.shape[0]

    def kernel(owners_ref, *refs):
        piece_refs, grads_ref, refs = refs[: len(pieces)], refs[len(pieces)], refs[len(pieces) + 1 :]
        out_refs, (whole_ref, held_ref, sems) = refs[:-3], refs[-3:]
        step = pl.program_id(0)

        def fetch(block):
            return pltpu.make_async_copy(grads_ref.at[owners_ref[block]], held_ref.at[block], sems.at[block])

        @pl.when(step == 0)
        def _():
            for block in range(count):
                fetch(block).start()
            for index, piece_ref in enumerate(piece_refs):
                row, column = index % 2 * rows, index // 2 * run
                whole_ref[row : row + rows, column : column + run] = piece_ref[...]

        fetch(step).wait()
        value = jnp.dot(held_ref[step], whole_ref[...], preferred_element_type=F32).astype(BF16)
        for out_ref, cut in zip(out_refs, cuts):
            out_ref[0] = value[cut]

    shapes = [(cut[0].stop - cut[0].start, cut[1].stop - cut[1].start) for cut in cuts]
    return pl.pallas_call(
        kernel,
        out_shape=[jax.ShapeDtypeStruct((count, *shape), BF16) for shape in shapes],
        grid_spec=pltpu.PrefetchScalarGridSpec(
            num_scalar_prefetch=1,
            grid=(count,),
            in_specs=[pl.BlockSpec((rows, run), lambda i, owners_ref: (0, 0))] * len(pieces)
            + [pl.BlockSpec(memory_space=pl.ANY)],
            out_specs=[pl.BlockSpec((1, *shape), lambda i, owners_ref: (i, 0, 0)) for shape in shapes],
            scratch_shapes=[
                pltpu.VMEM((tokens, width), BF16),
                pltpu.VMEM((count, owned, tokens), BF16),
                pltpu.SemaphoreType.DMA((count,)),
            ],
        ),
        compiler_params=RING_PARAMS,
        cost_estimate=COST,
        name="gradient",
    )(owners, *pieces, grads_t)


def accumulate(arrived, own, coming, hop):
    _, rows, width = own.shape

    def kernel(*refs):
        total = refs[0][0].astype(F32) + refs[1][0].astype(F32)
        if arrived:
            total = total + refs[2][...].astype(F32)
        refs[-1][...] = total.astype(BF16)

    block = pl.BlockSpec((1, rows, width), lambda i: (hop, 0, 0))
    return pl.pallas_call(
        kernel,
        grid=(1,),
        out_shape=jax.ShapeDtypeStruct((rows, width), BF16),
        in_specs=[block, block] + [pl.BlockSpec(memory_space=pltpu.VMEM)] * len(arrived),
        out_specs=pl.BlockSpec(memory_space=pltpu.VMEM),
        compiler_params=RING_PARAMS,
        cost_estimate=COST,
        name="accumulate",
    )(own, coming, *arrived)


def adam(pieces, first, second, held, begin):
    owned, rank = first.shape
    count, rows, _ = pieces[0][1].shape
    widths = [piece[0].shape[1] for piece in pieces]
    width = sum(widths)

    def kernel(*refs):
        first_ref, second_ref = refs[3 * len(pieces) : 3 * len(pieces) + 2]
        first_out, second_out, direction_out = refs[-3:]
        at = 0
        for index, size in enumerate(widths):
            arrived_ref, own_ref, other_ref = refs[3 * index : 3 * index + 3]
            columns = slice(at, at + size)
            at += size
            grad_low = arrived_ref[...].astype(F32) + own_ref[0].astype(F32) + other_ref[0].astype(F32)
            first_next = beta_first * first_ref[:, columns] + (1.0 - beta_first) * grad_low
            second_next = beta_second * second_ref[:, columns] + (1.0 - beta_second) * grad_low * grad_low
            first_out[:, columns] = first_next
            second_out[:, columns] = second_next
            bias_first = 1.0 - beta_first**adam_count
            bias_second = 1.0 - beta_second**adam_count
            direction = first_next / bias_first / (jnp.sqrt(second_next / bias_second) + epsilon)
            direction_out[:, columns] = direction.astype(BF16)

    rectangle = pl.BlockSpec((pl.Element(rows), pl.Element(width)), lambda i: begin)
    piece_specs = []
    for size in widths:
        piece_specs += [pl.BlockSpec(memory_space=pltpu.VMEM)]
        piece_specs += [pl.BlockSpec((1, rows, size), lambda i: (count - 1, 0, 0))] * 2
    inputs = len(piece_specs) + 2
    return pl.pallas_call(
        kernel,
        grid=(1,),
        out_shape=[
            jax.ShapeDtypeStruct((owned, rank), F32),
            jax.ShapeDtypeStruct((owned, rank), F32),
            jax.ShapeDtypeStruct((rows, width), BF16),
        ],
        in_specs=piece_specs + [rectangle, rectangle] + [pl.BlockSpec(memory_space=pl.ANY)] * len(held),
        out_specs=[rectangle, rectangle, pl.BlockSpec((rows, width), lambda i: (0, 0))],
        input_output_aliases={inputs + index: index for index in range(len(held))},
        compiler_params=RING_PARAMS,
        cost_estimate=COST,
        name="adam",
    )(*[array for piece in pieces for array in piece], first, second, *held)


def expand(targets, starts, rests, begin, basis_t, held, owned):
    rows, width = rests[0].shape
    rank, features = basis_t.shape
    count = len(starts)
    block = min(512, features)

    def kernel(targets_ref, basis_ref, *refs):
        start_refs, rest_refs = refs[:count], refs[count : 2 * count]
        out_ref, whole_ref = refs[-2:]

        @pl.when(pl.program_id(0) == 0)
        def _():
            for index in range(count):
                whole_ref[index, :, : rank - width] = start_refs[index][...]
                whole_ref[index, :, rank - width :] = rest_refs[index][...]

        for index in range(count):
            out_ref[targets_ref[index]] = jnp.dot(whole_ref[index], basis_ref[...], preferred_element_type=F32)

    return pl.pallas_call(
        kernel,
        out_shape=jax.ShapeDtypeStruct((count, owned, features), F32),
        grid_spec=pltpu.PrefetchScalarGridSpec(
            num_scalar_prefetch=1,
            grid=(features // block,),
            in_specs=[pl.BlockSpec((rank, block), lambda i, targets_ref: (0, i))]
            + [pl.BlockSpec((pl.Element(rows), pl.Element(rank - width)), lambda i, targets_ref: (begin, 0))] * count
            + [pl.BlockSpec((rows, width), lambda i, targets_ref: (0, 0))] * count
            + [pl.BlockSpec(memory_space=pl.ANY)] * len(held),
            out_specs=pl.BlockSpec(
                (pl.Element(count), pl.Element(rows), pl.Element(block)),
                lambda i, targets_ref: (0, begin, i * block),
            ),
            scratch_shapes=[pltpu.VMEM((count, rows, rank), BF16)],
        ),
        input_output_aliases={2 + 2 * count: 0} if held else {},
        compiler_params=RING_PARAMS,
        cost_estimate=COST,
        name="expand",
    )(targets, basis_t, *starts, *rests, *held)


def total_of(*terms):
    total = terms[0].astype(F32)
    for term in terms[1:]:
        total = total + term.astype(F32)
    return total.astype(BF16)


def after(value, *earlier):
    return lax.optimization_barrier((value, *jax.tree.leaves(earlier)))[0]


def local(activations, out_grads, projector, first_moment, second_moment):
    owned = first_moment.shape[1]
    features = activations[0]
    basis = projector[0]
    rank = basis.shape[1]
    tokens = features.shape[0]
    dp_count, fsdp_count = lax.axis_size("dp"), lax.axis_size("fsdp")
    dp, fsdp = lax.axis_index("dp"), lax.axis_index("fsdp")
    chips = dp_count // 2
    chip, core = dp // 2, dp % 2
    width = rank // 4

    offsets = [1 << bit for bit in range(fsdp_count.bit_length() - 1)]
    order = jnp.stack([fsdp ^ offset for offset in range(fsdp_count)]).astype(jnp.int32)
    hops = chips - 1
    ring_order = (chip - 1 - jnp.arange(chips, dtype=jnp.int32) + chips) % chips
    own_owners = (ring_order * 2 + core).astype(jnp.int32)
    other_owners = (ring_order * 2 + 1 - core).astype(jnp.int32)

    def across(value, offset):
        return lax.ppermute(value, "fsdp", [(index, index ^ offset) for index in range(fsdp_count)])

    def sibling(value):
        return lax.ppermute(value, "dp", [(index, index ^ 1) for index in range(dp_count)])

    def onward(value):
        return lax.ppermute(value, "dp", [(index, (index + 2) % dp_count) for index in range(dp_count)])

    def exchange(halves, step):
        return [across(half, offsets[step if index % 2 == 0 else -1 - step]) for index, half in enumerate(halves)]

    def add(halves, arrived, plus=total_of):
        return [plus(half, term) for half, term in zip(halves, arrived)]

    partial = jnp.dot(features, basis, preferred_element_type=F32).astype(BF16)
    low, high = partial[: tokens // 2], partial[tokens // 2 :]
    sums_0 = [low[:, :width], high[:, :width]]
    middle = (width + rank) // 2
    sums_1 = [half[:, run] for run in (slice(width, middle), slice(middle, rank)) for half in (low, high)]
    coming_0 = exchange(sums_0, 0)
    block = tokens // 4
    grads_t = transpose(after(out_grads[0], *sums_0), block, 0, 2)
    sums_0 = add(sums_0, [after(term, grads_t) for term in coming_0])
    for step in range(1, len(offsets) - 1):
        sums_0 = add(sums_0, exchange(sums_0, step))
    coming_0 = exchange(sums_0, len(offsets) - 1)
    grads_t = transpose(after(out_grads[0], *sums_0), block, 2, 2, (grads_t,)).reshape(dp_count, owned, tokens)
    sums_0 = add(sums_0, [after(term, grads_t) for term in coming_0])
    coming_1 = exchange([after(half, *sums_0) for half in sums_1], 0)

    cuts_0 = [(slice(0, owned), slice(0, width))]
    ends = [0, owned]
    if owned % 16 == 0:
        ends = [-(-owned * index // 48) * 16 for index in range(4)]
    rows_1 = [slice(*pair) for pair in zip(ends, ends[1:])]
    cuts_1 = [(rows, slice(0, rank - width)) for rows in rows_1]

    def ring(parts, stride, token, between, finish):
        events = sorted(
            (2 * hop + stride * part, part, hop)
            for part in range(len(parts))
            for hop in range(hops + (finish is not None))
        )
        arrived = [None] * len(parts)
        for number, (_, part, hop) in enumerate(events):
            if hop == hops:
                token = finish(part, after(arrived[part], token))
            else:
                own, coming = parts[part]
                before = () if arrived[part] is None else (arrived[part],)
                token = accumulate(before, after(own, token), coming, hop)
                arrived[part] = onward(token)
            if number in between:
                token = between[number](token)
        return token, arrived

    held = ()
    directions = []

    def step_of(pieces, begin):
        nonlocal held
        first_next, second_next, direction = adam(pieces, first_moment[0], second_moment[0], held, begin)
        held = (first_next, second_next)
        directions.append([direction])
        return direction

    def gather(part, *earlier):
        sent = after(directions[part][0], *earlier) if earlier else directions[part][0]
        directions[part] += [across(sent, offset) for offset in range(1, fsdp_count)]

    other = gradient(grads_t, sums_0, other_owners, cuts_0)
    coming = [sibling(value) for value in other]
    own = gradient(after(grads_t, *other), sums_0, own_owners, cuts_0)
    parts_0 = list(zip(own, coming))
    rest = {}

    def second_exchange(token):
        sums = add(sums_1, [after(term, token) for term in coming_1], plus)
        for step in range(1, len(offsets) - 1):
            sums = add(sums, exchange(sums, step), plus)
        rest["sums"], rest["coming"] = sums, exchange(sums, len(offsets) - 1)
        return sums[1]

    def start_rest(token):
        sums = add(rest["sums"], [after(term, token) for term in rest["coming"]], plus)
        rest["sums"] = sums
        rest["other"] = gradient(grads_t, sums, other_owners, cuts_1)
        return rest["other"][0]

    token, last_0 = ring(parts_0, 1, own[0], {0: second_exchange, 1: start_rest}, None)
    coming = [sibling(after(value, token)) for value in rest["other"]]
    own = gradient(after(grads_t, token), rest["sums"], own_owners, cuts_1)
    parts_1 = list(zip(own, coming))
    pieces = [(after(value, own[0]), *part) for value, part in zip(last_0, parts_0)]
    token = step_of(pieces, (0, 0))

    def turn_basis(token):
        rest["basis_t"] = transpose(after(basis, token), min(512, basis.shape[0]))
        return rest["basis_t"]

    def send_first(token):
        gather(0, token)
        return token

    def have_first(token):
        return [token, *directions[0]]

    def finish_1(part, arrived):
        token = step_of([(arrived, *parts_1[part])], (rows_1[part].start, width))
        gather(part + 1, *(directions[part - 1] if part > 1 else ()))
        return token

    first_send, first_wait = (1, 4)
    between = {2: turn_basis, first_send: send_first, first_wait: have_first}
    token, _ = ring(parts_1, 1.5, token, between, finish_1)

    update = ()
    for rows, gathered in zip(rows_1, directions[1:]):
        gathered = [after(gathered[0], token), *gathered[1:]]
        update = (expand(order, directions[0], gathered, rows.start, rest["basis_t"], update, owned),)
    return (update[0][None], held[0][None], held[1][None])


def solution(mesh):
    in_specs = (
        P(None, "dp", "fsdp"),
        P(None, "dp", "fsdp"),
        P(None, "fsdp", None),
        P(None, ("fsdp", "dp"), None),
        P(None, ("fsdp", "dp"), None),
    )
    out_specs = (
        P(None, None, "dp", "fsdp"),
        P(None, ("fsdp", "dp"), None),
        P(None, ("fsdp", "dp"), None),
    )
    return jax.shard_map(local, mesh=mesh, in_specs=in_specs, out_specs=out_specs, check_vma=False)
```

```python
import functools

import jax
import jax.numpy as jnp
from jax import lax
from jax.experimental import pallas as pl
from jax.experimental.pallas import tpu as pltpu
from jax.sharding import PartitionSpec as P

beta_first = 0.9
beta_second = 0.999
adam_count = 100.0
epsilon = 1e-08

F32 = jnp.float32
BF16 = jnp.bfloat16
COST = pl.CostEstimate(flops=1024, bytes_accessed=1 << 20, transcendentals=0)
PARAMS = pltpu.CompilerParams(vmem_limit_bytes=58 * 1024 * 1024)
RING_PARAMS = pltpu.CompilerParams(vmem_limit_bytes=64 * 1024 * 1024)


def transpose(value, block, begin=0, count=None, held=(), params=PARAMS):
    rows, columns = value.shape
    count = rows // block if count is None else count

    def kernel(value_ref, *refs):
        refs[-1][...] = value_ref[...].T

    return pl.pallas_call(
        kernel,
        out_shape=jax.ShapeDtypeStruct((columns, rows), value.dtype),
        grid=(count,),
        in_specs=[pl.BlockSpec((block, columns), lambda i: (begin + i, 0))]
        + [pl.BlockSpec(memory_space=pl.ANY)] * len(held),
        out_specs=pl.BlockSpec((columns, block), lambda i: (0, begin + i)),
        input_output_aliases={1: 0} if held else {},
        compiler_params=params,
        cost_estimate=COST,
        name="transpose",
    )(value, *held)


def plus(ones, twos):
    rows, width = ones[0].shape
    block = pl.BlockSpec((rows // 2, width), lambda i: (i, 0))
    count = len(ones)

    def kernel(*refs):
        for one_ref, two_ref, out_ref in zip(refs, refs[count:], refs[2 * count :]):
            out_ref[...] = (one_ref[...].astype(F32) + two_ref[...].astype(F32)).astype(BF16)

    return pl.pallas_call(
        kernel,
        grid=(2,),
        out_shape=[jax.ShapeDtypeStruct((rows, width), BF16)] * count,
        in_specs=[block] * (2 * count),
        out_specs=[block] * count,
        compiler_params=RING_PARAMS,
        cost_estimate=COST,
        name="plus",
    )(*ones, *twos)


def gradient(grads_t, pieces, owners, cuts):
    _, owned, tokens = grads_t.shape
    rows, run = pieces[0].shape
    width = run * len(pieces) // 2
    count = owners.shape[0]

    def kernel(owners_ref, *refs):
        piece_refs, grads_ref, refs = refs[: len(pieces)], refs[len(pieces)], refs[len(pieces) + 1 :]
        out_refs, (whole_ref, held_ref, sems) = refs[:-3], refs[-3:]
        step = pl.program_id(0)

        def fetch(block):
            return pltpu.make_async_copy(grads_ref.at[owners_ref[block]], held_ref.at[block], sems.at[block])

        @pl.when(step == 0)
        def _():
            for block in range(count):
                fetch(block).start()
            for index, piece_ref in enumerate(piece_refs):
                row, column = index % 2 * rows, index // 2 * run
                whole_ref[row : row + rows, column : column + run] = piece_ref[...]

        fetch(step).wait()
        value = jnp.dot(held_ref[step], whole_ref[...], preferred_element_type=F32).astype(BF16)
        for out_ref, cut in zip(out_refs, cuts):
            out_ref[0] = value[cut]

    shapes = [(cut[0].stop - cut[0].start, cut[1].stop - cut[1].start) for cut in cuts]
    return pl.pallas_call(
        kernel,
        out_shape=[jax.ShapeDtypeStruct((count, *shape), BF16) for shape in shapes],
        grid_spec=pltpu.PrefetchScalarGridSpec(
            num_scalar_prefetch=1,
            grid=(count,),
            in_specs=[pl.BlockSpec((rows, run), lambda i, owners_ref: (0, 0))] * len(pieces)
            + [pl.BlockSpec(memory_space=pl.ANY)],
            out_specs=[pl.BlockSpec((1, *shape), lambda i, owners_ref: (i, 0, 0)) for shape in shapes],
            scratch_shapes=[
                pltpu.VMEM((tokens, width), BF16),
                pltpu.VMEM((count, owned, tokens), BF16),
                pltpu.SemaphoreType.DMA((count,)),
            ],
        ),
        compiler_params=RING_PARAMS,
        cost_estimate=COST,
        name="gradient",
    )(owners, *pieces, grads_t)


def accumulate(places, arrived, own, coming, hop):
    _, rows, width = own.shape

    def kernel(places_ref, own_ref, coming_ref, *refs):
        total = own_ref[0].astype(F32) + coming_ref[0].astype(F32)
        if arrived:
            total = total + refs[0][...].astype(F32)
        refs[-1][...] = total.astype(BF16)

    return pl.pallas_call(
        kernel,
        out_shape=jax.ShapeDtypeStruct((rows, width), BF16),
        grid_spec=pltpu.PrefetchScalarGridSpec(
            num_scalar_prefetch=1,
            grid=(1,),
            in_specs=[
                pl.BlockSpec((1, rows, width), lambda i, places_ref: (places_ref[0, hop], 0, 0)),
                pl.BlockSpec((1, rows, width), lambda i, places_ref: (places_ref[1, hop], 0, 0)),
            ]
            + [pl.BlockSpec(memory_space=pltpu.VMEM)] * len(arrived),
            out_specs=pl.BlockSpec(memory_space=pltpu.VMEM),
        ),
        compiler_params=RING_PARAMS,
        cost_estimate=COST,
        name="accumulate",
    )(places, own, coming, *arrived)


def adam(places, arrived, own, coming, first, second, held, begin):
    owned, rank = first.shape
    rows, width = arrived.shape
    last = places.shape[1] - 1

    def kernel(places_ref, arrived_ref, own_ref, coming_ref, first_ref, second_ref, *refs):
        first_out, second_out, direction_out = refs[-3:]
        grad_low = arrived_ref[...].astype(F32) + own_ref[0].astype(F32) + coming_ref[0].astype(F32)
        first_next = beta_first * first_ref[...] + (1.0 - beta_first) * grad_low
        second_next = beta_second * second_ref[...] + (1.0 - beta_second) * grad_low * grad_low
        first_out[...] = first_next
        second_out[...] = second_next
        bias_first = 1.0 - beta_first**adam_count
        bias_second = 1.0 - beta_second**adam_count
        direction = first_next / bias_first / (jnp.sqrt(second_next / bias_second) + epsilon)
        direction_out[...] = direction.astype(BF16)

    rectangle = pl.BlockSpec((pl.Element(rows), pl.Element(width)), lambda i, places_ref: begin)
    return pl.pallas_call(
        kernel,
        out_shape=[
            jax.ShapeDtypeStruct((owned, rank), F32),
            jax.ShapeDtypeStruct((owned, rank), F32),
            jax.ShapeDtypeStruct((rows, width), BF16),
        ],
        grid_spec=pltpu.PrefetchScalarGridSpec(
            num_scalar_prefetch=1,
            grid=(1,),
            in_specs=[
                pl.BlockSpec(memory_space=pltpu.VMEM),
                pl.BlockSpec((1, rows, width), lambda i, places_ref: (places_ref[0, last], 0, 0)),
                pl.BlockSpec((1, rows, width), lambda i, places_ref: (places_ref[1, last], 0, 0)),
                rectangle,
                rectangle,
            ]
            + [pl.BlockSpec(memory_space=pl.ANY)] * len(held),
            out_specs=[rectangle, rectangle, pl.BlockSpec((rows, width), lambda i, places_ref: (0, 0))],
        ),
        input_output_aliases={6 + index: index for index in range(len(held))},
        compiler_params=RING_PARAMS,
        cost_estimate=COST,
        name="adam",
    )(places, arrived, own, coming, first, second, *held)


def expand(targets, starts, rests, begin, basis_t, held, owned):
    rows, width = rests[0].shape
    rank, features = basis_t.shape
    count = len(starts)
    block = min(512, features)

    def kernel(targets_ref, basis_ref, *refs):
        start_refs, rest_refs = refs[:count], refs[count : 2 * count]
        out_ref, whole_ref = refs[-2:]

        @pl.when(pl.program_id(0) == 0)
        def _():
            for index in range(count):
                here = slice(index * rows, (index + 1) * rows)
                whole_ref[here, : rank - width] = start_refs[index][...]
                whole_ref[here, rank - width :] = rest_refs[index][...]

        value = jnp.dot(whole_ref[...], basis_ref[...], preferred_element_type=F32)
        for index in range(count):
            out_ref[targets_ref[index]] = value[index * rows : (index + 1) * rows]

    return pl.pallas_call(
        kernel,
        out_shape=jax.ShapeDtypeStruct((count, owned, features), F32),
        grid_spec=pltpu.PrefetchScalarGridSpec(
            num_scalar_prefetch=1,
            grid=(features // block,),
            in_specs=[pl.BlockSpec((rank, block), lambda i, targets_ref: (0, i))]
            + [pl.BlockSpec((pl.Element(rows), pl.Element(rank - width)), lambda i, targets_ref: (begin, 0))] * count
            + [pl.BlockSpec((rows, width), lambda i, targets_ref: (0, 0))] * count
            + [pl.BlockSpec(memory_space=pl.ANY)] * len(held),
            out_specs=pl.BlockSpec(
                (pl.Element(count), pl.Element(rows), pl.Element(block)),
                lambda i, targets_ref: (0, begin, i * block),
            ),
            scratch_shapes=[pltpu.VMEM((count * rows, rank), BF16)],
        ),
        input_output_aliases={2 + 2 * count: 0} if held else {},
        compiler_params=RING_PARAMS,
        cost_estimate=COST,
        name="expand",
    )(targets, basis_t, *starts, *rests, *held)


def total_of(*terms):
    total = terms[0].astype(F32)
    for term in terms[1:]:
        total = total + term.astype(F32)
    return total.astype(BF16)


def after(value, *earlier):
    return lax.optimization_barrier((value, *jax.tree.leaves(earlier)))[0]


def local(activations, out_grads, projector, first_moment, second_moment):
    owned = first_moment.shape[1]
    features = activations[0]
    basis = projector[0]
    rank = basis.shape[1]
    tokens = features.shape[0]
    dp_count, fsdp_count = lax.axis_size("dp"), lax.axis_size("fsdp")
    dp, fsdp = lax.axis_index("dp"), lax.axis_index("fsdp")
    chips = dp_count // 2
    chip, core = dp // 2, dp % 2
    width = rank // 4

    offsets = [1 << bit for bit in range(fsdp_count.bit_length() - 1)]
    order = jnp.stack([fsdp ^ offset for offset in range(fsdp_count)]).astype(jnp.int32)
    hops = chips - 1
    ring_order = (chip - 1 - jnp.arange(chips, dtype=jnp.int32) + chips) % chips
    own_owners = (ring_order * 2 + core).astype(jnp.int32)
    other_owners = (ring_order * 2 + 1 - core).astype(jnp.int32)

    def across(value, offset):
        return lax.ppermute(value, "fsdp", [(index, index ^ offset) for index in range(fsdp_count)])

    def sibling(value):
        return lax.ppermute(value, "dp", [(index, index ^ 1) for index in range(dp_count)])

    def onward(value):
        return lax.ppermute(value, "dp", [(index, (index + 2) % dp_count) for index in range(dp_count)])

    def exchange(halves, step):
        return [across(half, offsets[step if index % 2 == 0 else -1 - step]) for index, half in enumerate(halves)]

    def add(halves, arrived):
        return [total_of(half, term) for half, term in zip(halves, arrived)]

    def add_pairs(pieces, arrived):
        return [
            total
            for index in range(0, len(pieces), 2)
            for total in plus(pieces[index : index + 2], arrived[index : index + 2])
        ]

    def projected(features, columns):
        return [
            jnp.dot(half, basis[:, columns], preferred_element_type=F32).astype(BF16)
            for half in (features[: tokens // 2], features[tokens // 2 :])
        ]

    sums_0 = projected(features, slice(0, width))
    middle = (width + rank) // 2
    later = after(features, *sums_0)
    sums_1 = projected(later, slice(width, middle)) + projected(later, slice(middle, rank))
    coming_0 = exchange(sums_0, 0)
    block = tokens // 4
    grads_t = transpose(after(out_grads[0], *sums_1), block, 0, 2)
    sums_0 = add(sums_0, [after(term, grads_t) for term in coming_0])
    for step in range(1, len(offsets) - 1):
        sums_0 = add(sums_0, exchange(sums_0, step))
    coming_0 = exchange(sums_0, len(offsets) - 1)
    grads_t = transpose(after(out_grads[0], *sums_0), block, 2, 2, (grads_t,)).reshape(dp_count, owned, tokens)
    sums_0 = add(sums_0, [after(term, grads_t) for term in coming_0])
    coming_1 = exchange([after(half, *sums_0) for half in sums_1], 0)

    ends = [0, owned]
    if owned % 16 == 0:
        ends = [-(-owned * index // 48) * 16 for index in range(4)]
    rows_1 = [slice(*pair) for pair in zip(ends, ends[1:])]
    cuts_1 = [(rows, slice(0, rank - width)) for rows in rows_1]

    def ring(places, parts, stride, token, between, finish):
        events = sorted(
            (2 * hop + stride * part, part, hop)
            for part in range(len(parts))
            for hop in range(hops + (finish is not None))
        )
        arrived = [None] * len(parts)
        for number, (_, part, hop) in enumerate(events):
            if hop == hops:
                token = finish(part, after(arrived[part], token))
            else:
                own, coming = parts[part]
                before = () if arrived[part] is None else (arrived[part],)
                token = accumulate(places, before, after(own, token), coming, hop)
                arrived[part] = onward(token)
            if number in between:
                token = between[number](token)
        return token, arrived

    held = ()
    directions = []

    def step_of(places, arrived, part, begin):
        nonlocal held
        first_next, second_next, direction = adam(
            places, arrived, *part, first_moment[0], second_moment[0], held, begin
        )
        held = (first_next, second_next)
        directions.append([direction])
        return direction

    def gather(part, *earlier):
        sent = after(directions[part][0], *earlier) if earlier else directions[part][0]
        directions[part] += [across(sent, offset) for offset in range(1, fsdp_count)]

    whole = jnp.concatenate(sums_0)
    product = jnp.dot(grads_t.reshape(dp_count * owned, tokens), whole, preferred_element_type=F32).astype(BF16)
    pairs = product.reshape(chips, 2, owned, width)
    coming = sibling(lax.dynamic_slice_in_dim(pairs, 1 - core, 1, axis=1)[:, 0])
    part_0 = (product.reshape(dp_count, owned, width), coming)
    places_0 = jnp.stack([own_owners, ring_order])
    places_1 = jnp.stack([jnp.arange(chips, dtype=jnp.int32)] * 2)
    rest = {}

    def second_exchange(token):
        sums = add_pairs(sums_1, [after(term, token) for term in coming_1])
        for step in range(1, len(offsets) - 1):
            sums = add_pairs(sums, exchange(sums, step))
        rest["sums"], rest["coming"] = sums, exchange(sums, len(offsets) - 1)
        return sums[1]

    def start_rest(token):
        sums = add_pairs(rest["sums"], [after(term, token) for term in rest["coming"]])
        rest["sums"] = sums
        rest["other"] = gradient(grads_t, sums, other_owners, cuts_1)
        return rest["other"][0]

    token, last_0 = ring(places_0, [part_0], 1, product, {0: second_exchange, 1: start_rest}, None)
    coming = [sibling(after(value, token)) for value in rest["other"]]
    own = gradient(after(grads_t, token), rest["sums"], own_owners, cuts_1)
    parts_1 = list(zip(own, coming))

    def finish_0(token):
        direction = step_of(places_0, after(last_0[0], token), part_0, (0, 0))
        gather(0)
        return direction

    def turn_basis(token):
        rest["basis_t"] = transpose(after(basis, token), min(512, basis.shape[0]), params=RING_PARAMS)
        return rest["basis_t"]

    def have_first(token):
        return [token, *directions[0]]

    def finish_1(part, arrived):
        token = step_of(places_1, arrived, parts_1[part], (rows_1[part].start, width))
        gather(part + 1, *(directions[part - 1] if part > 1 else ()))
        return token

    between = {1: finish_0, 2: turn_basis, 4: have_first}
    token, _ = ring(places_1, parts_1, 1.5, [own[0], *last_0], between, finish_1)

    update = ()
    for rows, gathered in zip(rows_1, directions[1:]):
        gathered = [after(gathered[0], token), *gathered[1:]]
        update = (expand(order, directions[0], gathered, rows.start, rest["basis_t"], update, owned),)
    return (update[0][None], held[0][None], held[1][None])


def solution(mesh):
    in_specs = (
        P(None, "dp", "fsdp"),
        P(None, "dp", "fsdp"),
        P(None, "fsdp", None),
        P(None, ("fsdp", "dp"), None),
        P(None, ("fsdp", "dp"), None),
    )
    out_specs = (
        P(None, None, "dp", "fsdp"),
        P(None, ("fsdp", "dp"), None),
        P(None, ("fsdp", "dp"), None),
    )
    return jax.shard_map(local, mesh=mesh, in_specs=in_specs, out_specs=out_specs, check_vma=False)
```

```python
import functools

import jax
import jax.numpy as jnp
from jax import lax
from jax.experimental import pallas as pl
from jax.experimental.pallas import tpu as pltpu
from jax.sharding import PartitionSpec as P

beta_first = 0.9
beta_second = 0.999
adam_count = 100.0
epsilon = 1e-08

F32 = jnp.float32
BF16 = jnp.bfloat16
COST = pl.CostEstimate(flops=1024, bytes_accessed=1 << 20, transcendentals=0)
PARAMS = pltpu.CompilerParams(vmem_limit_bytes=58 * 1024 * 1024)
RING_PARAMS = pltpu.CompilerParams(vmem_limit_bytes=64 * 1024 * 1024)


def turn(core, grads, owned):
    tokens, columns = grads.shape
    chips = columns // (2 * owned)
    block = tokens // 4

    def kernel(core_ref, grads_ref, out_ref):
        for parity in range(2):

            @pl.when(core_ref[0] == parity)
            def _(parity=parity):
                for chip in range(chips):
                    begin = (2 * chip + parity) * owned
                    low = begin // 128 * 128
                    high = min(-(-(begin + owned) // 128) * 128, columns)
                    value = grads_ref[:, low:high].T
                    out_ref[chip] = value[begin - low : begin - low + owned]

    return pl.pallas_call(
        kernel,
        out_shape=jax.ShapeDtypeStruct((chips, owned, tokens), BF16),
        grid_spec=pltpu.PrefetchScalarGridSpec(
            num_scalar_prefetch=1,
            grid=(4,),
            in_specs=[pl.BlockSpec((block, columns), lambda i, core_ref: (i, 0))],
            out_specs=pl.BlockSpec((chips, owned, block), lambda i, core_ref: (0, 0, i)),
        ),
        compiler_params=PARAMS,
        cost_estimate=COST,
        name="turn",
    )(core, grads)


def plus(ones, twos, runs=1):
    rows, width = ones[0].shape
    count, size = len(ones), width // runs
    block = pl.BlockSpec((rows // 2, width), lambda i: (i, 0))

    def kernel(*refs):
        for index in range(count):
            total = (refs[index][...].astype(F32) + refs[count + index][...].astype(F32)).astype(BF16)
            for run in range(runs):
                refs[(2 + run) * count + index][...] = total[:, run * size : (run + 1) * size]

    return pl.pallas_call(
        kernel,
        grid=(2,),
        out_shape=[jax.ShapeDtypeStruct((rows, size), BF16)] * (count * runs),
        in_specs=[block] * (2 * count),
        out_specs=[pl.BlockSpec((rows // 2, size), lambda i: (i, 0))] * (count * runs),
        compiler_params=RING_PARAMS,
        cost_estimate=COST,
        name="plus",
    )(*ones, *twos)


def gradient(stacks, pieces, order, cuts=None):
    _, owned, tokens = stacks[0].shape
    rows, width = pieces[0].shape
    count = order.shape[0]

    def kernel(order_ref, *refs):
        piece_refs = refs[: len(pieces)]
        stack_refs = refs[len(pieces) : len(pieces) + 2]
        out_refs, (whole_ref, held_ref, sems) = refs[len(pieces) + 2 : -3], refs[-3:]
        step = pl.program_id(0)

        def fetch(block, side):
            return pltpu.make_async_copy(
                stack_refs[side].at[order_ref[block]],
                held_ref.at[block, :, pl.ds(side * tokens, tokens)],
                sems.at[block, side],
            )

        @pl.when(step == 0)
        def _():
            for block in range(count):
                for side in range(2):
                    fetch(block, side).start()
            for index, piece_ref in enumerate(piece_refs):
                whole_ref[index * rows : (index + 1) * rows, :] = piece_ref[...]

        for side in range(2):
            fetch(step, side).wait()
        value = jnp.dot(held_ref[step], whole_ref[...], preferred_element_type=F32).astype(BF16)
        if cuts is None:
            out_refs[0][0] = value
        else:
            for out_ref, cut in zip(out_refs, cuts):
                out_ref[...] = value[cut]

    if cuts is None:
        out_shape = [jax.ShapeDtypeStruct((count, owned, width), BF16)]
        out_specs = [pl.BlockSpec((1, owned, width), lambda i, order_ref: (i, 0, 0))]
    else:
        out_shape = [jax.ShapeDtypeStruct((cut.stop - cut.start, width), BF16) for cut in cuts]
        out_specs = [pl.BlockSpec(out.shape, lambda i, order_ref: (0, 0)) for out in out_shape]
    results = pl.pallas_call(
        kernel,
        out_shape=out_shape,
        grid_spec=pltpu.PrefetchScalarGridSpec(
            num_scalar_prefetch=1,
            grid=(count,),
            in_specs=[pl.BlockSpec((rows, width), lambda i, order_ref: (0, 0))] * len(pieces)
            + [pl.BlockSpec(memory_space=pl.ANY)] * 2,
            out_specs=out_specs,
            scratch_shapes=[
                pltpu.VMEM((2 * tokens, width), BF16),
                pltpu.VMEM((count, owned, 2 * tokens), BF16),
                pltpu.SemaphoreType.DMA((count, 2)),
            ],
        ),
        compiler_params=RING_PARAMS,
        cost_estimate=COST,
        name="gradient",
    )(order, *pieces, *stacks)
    return results[0] if cuts is None else results


def part_of(stack, block, rows):
    shape = (pl.Element(1), pl.Element(rows.stop - rows.start), pl.Element(stack.shape[2]))
    return pl.BlockSpec(shape, lambda i: (block, rows.start, 0))


def accumulate(arrived, own, block, rows):
    def kernel(own_ref, arrived_ref, out_ref):
        out_ref[...] = (own_ref[0].astype(F32) + arrived_ref[...].astype(F32)).astype(BF16)

    return pl.pallas_call(
        kernel,
        grid=(1,),
        out_shape=jax.ShapeDtypeStruct(arrived.shape, BF16),
        in_specs=[part_of(own, block, rows), pl.BlockSpec(memory_space=pltpu.VMEM)],
        out_specs=pl.BlockSpec(memory_space=pltpu.VMEM),
        compiler_params=RING_PARAMS,
        cost_estimate=COST,
        name="accumulate",
    )(own, arrived)


def adam(arrived, stacks, block, rows, first, second, held, column):
    owned, rank = first.shape
    height, width = arrived.shape

    def kernel(arrived_ref, first_ref, second_ref, *refs):
        first_out, second_out, direction_out = refs[-3:]
        grad_low = arrived_ref[...].astype(F32)
        for stack_ref in refs[: len(stacks)]:
            grad_low = grad_low + stack_ref[0].astype(F32)
        first_next = beta_first * first_ref[...] + (1.0 - beta_first) * grad_low
        second_next = beta_second * second_ref[...] + (1.0 - beta_second) * grad_low * grad_low
        first_out[...] = first_next
        second_out[...] = second_next
        bias_first = 1.0 - beta_first**adam_count
        bias_second = 1.0 - beta_second**adam_count
        direction = first_next / bias_first / (jnp.sqrt(second_next / bias_second) + epsilon)
        direction_out[...] = direction.astype(BF16)

    rectangle = pl.BlockSpec((pl.Element(height), pl.Element(width)), lambda i: (rows.start, column))
    return pl.pallas_call(
        kernel,
        grid=(1,),
        out_shape=[
            jax.ShapeDtypeStruct((owned, rank), F32),
            jax.ShapeDtypeStruct((owned, rank), F32),
            jax.ShapeDtypeStruct((height, width), BF16),
        ],
        in_specs=[pl.BlockSpec(memory_space=pltpu.VMEM), rectangle, rectangle]
        + [part_of(stack, block, rows) for stack in stacks]
        + [pl.BlockSpec(memory_space=pl.ANY)] * len(held),
        out_specs=[rectangle, rectangle, pl.BlockSpec((height, width), lambda i: (0, 0))],
        input_output_aliases={3 + len(stacks) + index: index for index in range(len(held))},
        compiler_params=RING_PARAMS,
        cost_estimate=COST,
        name="adam",
    )(arrived, first, second, *stacks, *held)


def expand(targets, starts, rests, rows, owned, basis, held):
    count = len(starts)
    begin = starts[0].shape[1]
    height, width = rests[0].shape
    features, rank = basis.shape
    block = min(512, features)

    def kernel(targets_ref, basis_ref, *refs):
        start_refs, rest_refs, (out_ref, whole_ref) = refs[:count], refs[count : 2 * count], refs[-2:]

        @pl.when(pl.program_id(0) == 0)
        def _():
            for index in range(count):
                here = slice(index * height, (index + 1) * height)
                whole_ref[here, :begin] = start_refs[index][...]
                whole_ref[here, begin:] = rest_refs[index][...]

        value = lax.dot_general(
            whole_ref[...], basis_ref[...], (((1,), (1,)), ((), ())), preferred_element_type=F32
        )
        for index in range(count):
            out_ref[targets_ref[index]] = value[index * height : (index + 1) * height]

    return pl.pallas_call(
        kernel,
        out_shape=jax.ShapeDtypeStruct((count, owned, features), F32),
        grid_spec=pltpu.PrefetchScalarGridSpec(
            num_scalar_prefetch=1,
            grid=(features // block,),
            in_specs=[pl.BlockSpec((block, rank), lambda i, targets_ref: (i, 0))]
            + [pl.BlockSpec((height, begin), lambda i, targets_ref: (0, 0))] * count
            + [pl.BlockSpec((height, width), lambda i, targets_ref: (0, 0))] * count
            + [pl.BlockSpec(memory_space=pl.ANY)] * len(held),
            out_specs=pl.BlockSpec(
                (pl.Element(count), pl.Element(height), pl.Element(block)),
                lambda i, targets_ref: (0, rows.start, i * block),
            ),
            scratch_shapes=[pltpu.VMEM((count * height, rank), BF16)],
        ),
        input_output_aliases={2 + 2 * count: 0} if held else {},
        compiler_params=RING_PARAMS,
        cost_estimate=COST,
        name="expand",
    )(targets, basis, *starts, *rests, *held)


def total_of(*terms):
    total = terms[0].astype(F32)
    for term in terms[1:]:
        total = total + term.astype(F32)
    return total.astype(BF16)


def after(value, *earlier):
    return lax.optimization_barrier((value, *jax.tree.leaves(earlier)))[0]


def local(activations, out_grads, projector, first_moment, second_moment):
    owned = first_moment.shape[1]
    features = activations[0]
    basis = projector[0]
    rank = basis.shape[1]
    tokens = features.shape[0]
    dp_count, fsdp_count = lax.axis_size("dp"), lax.axis_size("fsdp")
    dp, fsdp = lax.axis_index("dp"), lax.axis_index("fsdp")
    chips = dp_count // 2
    chip, core = dp // 2, dp % 2
    width = rank * 3 // 8

    offsets = [1 << bit for bit in range(fsdp_count.bit_length() - 1)]
    order = jnp.stack([fsdp ^ offset for offset in range(fsdp_count)]).astype(jnp.int32)
    hops = chips - 1
    ring_order = (chip - 1 - jnp.arange(chips, dtype=jnp.int32) + chips) % chips

    def across(value, offset):
        return lax.ppermute(value, "fsdp", [(index, index ^ offset) for index in range(fsdp_count)])

    def sibling(value):
        return lax.ppermute(value, "dp", [(index, index ^ 1) for index in range(dp_count)])

    def onward(value):
        return lax.ppermute(value, "dp", [(index, (index + 2) % dp_count) for index in range(dp_count)])

    def exchange(halves, step):
        return [across(half, offsets[step if index % 2 == 0 else -1 - step]) for index, half in enumerate(halves)]

    def add(halves, arrived):
        return [total_of(half, term) for half, term in zip(halves, arrived)]

    def add_pairs(pieces, arrived):
        return [
            total
            for index in range(0, len(pieces), 2)
            for total in plus(pieces[index : index + 2], arrived[index : index + 2])
        ]

    def projected(features, columns):
        partial = jnp.dot(features, basis[:, columns], preferred_element_type=F32).astype(BF16)
        return [partial[: tokens // 2], partial[tokens // 2 :]]

    grads = out_grads[0]
    others_grads = sibling(grads)
    sums_0 = projected(features, slice(0, width))
    coming_0 = exchange(sums_0, 0)
    sums_1 = projected(after(features, *sums_0), slice(width, rank))
    parity = jnp.reshape(core, (1,)).astype(jnp.int32)
    mine = turn(parity, after(grads, *sums_1), owned)
    sums_0 = add(sums_0, [after(term, mine) for term in coming_0])
    for step in range(1, len(offsets) - 1):
        sums_0 = add(sums_0, exchange(sums_0, step))
    coming_0 = exchange(sums_0, len(offsets) - 1)
    theirs = turn(parity, after(others_grads, *sums_0), owned)
    stacks = [mine, theirs]
    sums_0 = add(sums_0, [after(term, theirs) for term in coming_0])
    both_0 = sums_0 + [sibling(half) for half in sums_0]
    coming_1 = exchange([after(half, *sums_0) for half in sums_1], 0)

    product = gradient(stacks, both_0, jnp.arange(chips, dtype=jnp.int32))
    lines = [list(range(parity, dp_count, 2)) for parity in range(2)]
    mine_0 = lax.psum_scatter(
        product.reshape(chips * owned, width), "dp", scatter_dimension=0, axis_index_groups=lines, tiled=True
    )

    sums_1 = add_pairs(sums_1, [after(term, product) for term in coming_1])
    for step in range(1, len(offsets)):
        sums_1 = add_pairs(sums_1, exchange(sums_1, step))
    both_1 = sums_1 + [sibling(half) for half in sums_1]

    held = ()

    def step_of(arrived, stacks, block, rows, column):
        nonlocal held
        first_next, second_next, direction = adam(
            arrived, stacks, block, rows, first_moment[0], second_moment[0], held, column
        )
        held = (first_next, second_next)
        return direction

    ends = [0, owned]
    if owned % 16 == 0:
        ends = [-(-owned * index // 48) * 16 for index in range(4)]
    parts = [slice(*pair) for pair in zip(ends, ends[1:])]
    count = len(parts)

    leaving = gradient(stacks, both_1, ring_order[:1], parts)
    arrived = [onward(value) for value in leaving]
    others = gradient([after(stacks[0], *leaving), stacks[1]], both_1, ring_order[1:])

    token = others
    directions = []

    starts = [[] for _ in parts]
    stages = [(part, step) for part in range(count) for step in range(len(offsets))]
    reached = []

    def spread(token):
        part, step = stages.pop(0)
        rows = parts[part]
        if step == 0:
            starts[part].append(step_of(after(mine_0[rows], token), (), 0, rows, 0))
        starts[part].extend([across(after(piece, token), offsets[step]) for piece in starts[part]])
        return starts[part]

    events = sorted((2 * hop + 1.5 * part, part, hop) for part in range(count) for hop in range(1, chips))
    for number, (_, part, hop) in enumerate(events):
        rows = parts[part]
        if number >= 2 and (reached or stages):
            token = [token, *reached]
            reached = spread(token) if stages else []
        if hop < hops:
            token = accumulate(after(arrived[part], token), others, hop - 1, rows)
            arrived[part] = onward(token)
            continue
        token = step_of(after(arrived[part], token), (others,), hop - 1, rows, width)
        sent = after(token, directions[part - 2]) if part > 1 else token
        directions.append([token] + [across(sent, offset) for offset in range(1, fsdp_count)])
    while stages:
        spread(token)

    update = ()
    for rows, start, pieces in zip(parts, starts, directions):
        pieces = [after(pieces[0], token), *pieces[1:]]
        update = (expand(order, start, pieces, rows, owned, basis, update),)
    return (update[0][None], held[0][None], held[1][None])


def solution(mesh):
    in_specs = (
        P(None, "dp", "fsdp"),
        P(None, "dp", "fsdp"),
        P(None, "fsdp", None),
        P(None, ("fsdp", "dp"), None),
        P(None, ("fsdp", "dp"), None),
    )
    out_specs = (
        P(None, None, "dp", "fsdp"),
        P(None, ("fsdp", "dp"), None),
        P(None, ("fsdp", "dp"), None),
    )
    return jax.shard_map(local, mesh=mesh, in_specs=in_specs, out_specs=out_specs, check_vma=False)
```

```python
import functools

import jax
import jax.numpy as jnp
from jax import lax
from jax.experimental import pallas as pl
from jax.experimental.pallas import tpu as pltpu
from jax.sharding import PartitionSpec as P

beta_first = 0.9
beta_second = 0.999
adam_count = 100.0
epsilon = 1e-08

F32 = jnp.float32
BF16 = jnp.bfloat16
COST = pl.CostEstimate(flops=1024, bytes_accessed=1 << 20, transcendentals=0)
PARAMS = pltpu.CompilerParams(vmem_limit_bytes=58 * 1024 * 1024)
RING_PARAMS = pltpu.CompilerParams(vmem_limit_bytes=64 * 1024 * 1024)


def turn(core, grads, owned):
    tokens, columns = grads.shape
    chips = columns // (2 * owned)
    block = tokens // 4

    def kernel(core_ref, grads_ref, out_ref):
        for parity in range(2):

            @pl.when(core_ref[0] == parity)
            def _(parity=parity):
                for chip in range(chips):
                    begin = (2 * chip + parity) * owned
                    low = begin // 128 * 128
                    high = min(-(-(begin + owned) // 128) * 128, columns)
                    value = grads_ref[:, low:high].T
                    out_ref[chip] = value[begin - low : begin - low + owned]

    return pl.pallas_call(
        kernel,
        out_shape=jax.ShapeDtypeStruct((chips, owned, tokens), BF16),
        grid_spec=pltpu.PrefetchScalarGridSpec(
            num_scalar_prefetch=1,
            grid=(4,),
            in_specs=[pl.BlockSpec((block, columns), lambda i, core_ref: (i, 0))],
            out_specs=pl.BlockSpec((chips, owned, block), lambda i, core_ref: (0, 0, i)),
        ),
        compiler_params=PARAMS,
        cost_estimate=COST,
        name="turn",
    )(core, grads)


def plus(ones, twos, runs=1):
    rows, width = ones[0].shape
    count, size = len(ones), width // runs
    block = pl.BlockSpec((rows // 2, width), lambda i: (i, 0))

    def kernel(*refs):
        for index in range(count):
            total = (refs[index][...].astype(F32) + refs[count + index][...].astype(F32)).astype(BF16)
            for run in range(runs):
                refs[(2 + run) * count + index][...] = total[:, run * size : (run + 1) * size]

    return pl.pallas_call(
        kernel,
        grid=(2,),
        out_shape=[jax.ShapeDtypeStruct((rows, size), BF16)] * (count * runs),
        in_specs=[block] * (2 * count),
        out_specs=[pl.BlockSpec((rows // 2, size), lambda i: (i, 0))] * (count * runs),
        compiler_params=RING_PARAMS,
        cost_estimate=COST,
        name="plus",
    )(*ones, *twos)


def gradient(stacks, pieces, order, cuts=None):
    _, owned, tokens = stacks[0].shape
    rows, run = pieces[0].shape
    width = run * len(pieces) // 4
    count = order.shape[0]

    def kernel(order_ref, *refs):
        piece_refs = refs[: len(pieces)]
        stack_refs = refs[len(pieces) : len(pieces) + 2]
        out_refs, (whole_ref, held_ref, sems) = refs[len(pieces) + 2 : -3], refs[-3:]
        step = pl.program_id(0)

        def fetch(block, side):
            return pltpu.make_async_copy(
                stack_refs[side].at[order_ref[block]],
                held_ref.at[block, :, pl.ds(side * tokens, tokens)],
                sems.at[block, side],
            )

        @pl.when(step == 0)
        def _():
            for block in range(count):
                for side in range(2):
                    fetch(block, side).start()
            for index, piece_ref in enumerate(piece_refs):
                side, place = divmod(index, len(pieces) // 2)
                row, column = side * tokens + place % 2 * rows, place // 2 * run
                whole_ref[row : row + rows, column : column + run] = piece_ref[...]

        for side in range(2):
            fetch(step, side).wait()
        value = jnp.dot(held_ref[step], whole_ref[...], preferred_element_type=F32).astype(BF16)
        if cuts is None:
            out_refs[0][0] = value
        else:
            for out_ref, cut in zip(out_refs, cuts):
                out_ref[...] = value[cut]

    if cuts is None:
        out_shape = [jax.ShapeDtypeStruct((count, owned, width), BF16)]
        out_specs = [pl.BlockSpec((1, owned, width), lambda i, order_ref: (i, 0, 0))]
    else:
        out_shape = [jax.ShapeDtypeStruct((cut.stop - cut.start, width), BF16) for cut in cuts]
        out_specs = [pl.BlockSpec(out.shape, lambda i, order_ref: (0, 0)) for out in out_shape]
    results = pl.pallas_call(
        kernel,
        out_shape=out_shape,
        grid_spec=pltpu.PrefetchScalarGridSpec(
            num_scalar_prefetch=1,
            grid=(count,),
            in_specs=[pl.BlockSpec((rows, run), lambda i, order_ref: (0, 0))] * len(pieces)
            + [pl.BlockSpec(memory_space=pl.ANY)] * 2,
            out_specs=out_specs,
            scratch_shapes=[
                pltpu.VMEM((2 * tokens, width), BF16),
                pltpu.VMEM((count, owned, 2 * tokens), BF16),
                pltpu.SemaphoreType.DMA((count, 2)),
            ],
        ),
        compiler_params=RING_PARAMS,
        cost_estimate=COST,
        name="gradient",
    )(order, *pieces, *stacks)
    return results[0] if cuts is None else results


def part_of(stack, block, rows):
    shape = (pl.Element(1), pl.Element(rows.stop - rows.start), pl.Element(stack.shape[2]))
    return pl.BlockSpec(shape, lambda i: (block, rows.start, 0))


def accumulate(arrived, own, block, rows):
    def kernel(own_ref, arrived_ref, out_ref):
        out_ref[...] = (own_ref[0].astype(F32) + arrived_ref[...].astype(F32)).astype(BF16)

    return pl.pallas_call(
        kernel,
        grid=(1,),
        out_shape=jax.ShapeDtypeStruct(arrived.shape, BF16),
        in_specs=[part_of(own, block, rows), pl.BlockSpec(memory_space=pltpu.VMEM)],
        out_specs=pl.BlockSpec(memory_space=pltpu.VMEM),
        compiler_params=RING_PARAMS,
        cost_estimate=COST,
        name="accumulate",
    )(own, arrived)


def adam(arrived, stack, block, rows, first, second, held, column):
    owned, rank = first.shape
    height, width = arrived.shape

    def kernel(arrived_ref, stack_ref, first_ref, second_ref, *refs):
        first_out, second_out, direction_out = refs[-3:]
        grad_low = arrived_ref[...].astype(F32) + stack_ref[0].astype(F32)
        first_next = beta_first * first_ref[...] + (1.0 - beta_first) * grad_low
        second_next = beta_second * second_ref[...] + (1.0 - beta_second) * grad_low * grad_low
        first_out[...] = first_next
        second_out[...] = second_next
        bias_first = 1.0 - beta_first**adam_count
        bias_second = 1.0 - beta_second**adam_count
        direction = first_next / bias_first / (jnp.sqrt(second_next / bias_second) + epsilon)
        direction_out[...] = direction.astype(BF16)

    rectangle = pl.BlockSpec((pl.Element(height), pl.Element(width)), lambda i: (rows.start, column))
    return pl.pallas_call(
        kernel,
        grid=(1,),
        out_shape=[
            jax.ShapeDtypeStruct((owned, rank), F32),
            jax.ShapeDtypeStruct((owned, rank), F32),
            jax.ShapeDtypeStruct((height, width), BF16),
        ],
        in_specs=[pl.BlockSpec(memory_space=pltpu.VMEM), part_of(stack, block, rows), rectangle, rectangle]
        + [pl.BlockSpec(memory_space=pl.ANY)] * len(held),
        out_specs=[rectangle, rectangle, pl.BlockSpec((height, width), lambda i: (0, 0))],
        input_output_aliases={4 + index: index for index in range(len(held))},
        compiler_params=RING_PARAMS,
        cost_estimate=COST,
        name="adam",
    )(arrived, stack, first, second, *held)


def expand(targets, starts, rests, rows, basis, held):
    count = len(starts)
    owned, begin = starts[0].shape
    height, width = rests[0].shape
    features, rank = basis.shape
    block = min(512, features)

    def kernel(targets_ref, basis_ref, *refs):
        start_refs, rest_refs, (out_ref, whole_ref) = refs[:count], refs[count : 2 * count], refs[-2:]

        @pl.when(pl.program_id(0) == 0)
        def _():
            for index in range(count):
                here = slice(index * height, (index + 1) * height)
                whole_ref[here, :begin] = start_refs[index][...]
                whole_ref[here, begin:] = rest_refs[index][...]

        value = lax.dot_general(
            whole_ref[...], basis_ref[...], (((1,), (1,)), ((), ())), preferred_element_type=F32
        )
        for index in range(count):
            out_ref[targets_ref[index]] = value[index * height : (index + 1) * height]

    return pl.pallas_call(
        kernel,
        out_shape=jax.ShapeDtypeStruct((count, owned, features), F32),
        grid_spec=pltpu.PrefetchScalarGridSpec(
            num_scalar_prefetch=1,
            grid=(features // block,),
            in_specs=[pl.BlockSpec((block, rank), lambda i, targets_ref: (i, 0))]
            + [pl.BlockSpec((pl.Element(height), pl.Element(begin)), lambda i, targets_ref: (rows.start, 0))] * count
            + [pl.BlockSpec((height, width), lambda i, targets_ref: (0, 0))] * count
            + [pl.BlockSpec(memory_space=pl.ANY)] * len(held),
            out_specs=pl.BlockSpec(
                (pl.Element(count), pl.Element(height), pl.Element(block)),
                lambda i, targets_ref: (0, rows.start, i * block),
            ),
            scratch_shapes=[pltpu.VMEM((count * height, rank), BF16)],
        ),
        input_output_aliases={2 + 2 * count: 0} if held else {},
        compiler_params=RING_PARAMS,
        cost_estimate=COST,
        name="expand",
    )(targets, basis, *starts, *rests, *held)


def total_of(*terms):
    total = terms[0].astype(F32)
    for term in terms[1:]:
        total = total + term.astype(F32)
    return total.astype(BF16)


def after(value, *earlier):
    return lax.optimization_barrier((value, *jax.tree.leaves(earlier)))[0]


def local(activations, out_grads, projector, first_moment, second_moment):
    owned = first_moment.shape[1]
    features = activations[0]
    basis = projector[0]
    rank = basis.shape[1]
    tokens = features.shape[0]
    dp_count, fsdp_count = lax.axis_size("dp"), lax.axis_size("fsdp")
    dp, fsdp = lax.axis_index("dp"), lax.axis_index("fsdp")
    chips = dp_count // 2
    chip, core = dp // 2, dp % 2
    width = rank // 4

    offsets = [1 << bit for bit in range(fsdp_count.bit_length() - 1)]
    order = jnp.stack([fsdp ^ offset for offset in range(fsdp_count)]).astype(jnp.int32)
    hops = chips - 1
    ring_order = (chip - 1 - jnp.arange(chips, dtype=jnp.int32) + chips) % chips

    def across(value, offset):
        return lax.ppermute(value, "fsdp", [(index, index ^ offset) for index in range(fsdp_count)])

    def sibling(value):
        return lax.ppermute(value, "dp", [(index, index ^ 1) for index in range(dp_count)])

    def onward(value):
        return lax.ppermute(value, "dp", [(index, (index + 2) % dp_count) for index in range(dp_count)])

    def exchange(halves, step):
        return [across(half, offsets[step if index % 2 == 0 else -1 - step]) for index, half in enumerate(halves)]

    def add(halves, arrived):
        return [total_of(half, term) for half, term in zip(halves, arrived)]

    def add_pairs(pieces, arrived):
        return [
            total
            for index in range(0, len(pieces), 2)
            for total in plus(pieces[index : index + 2], arrived[index : index + 2])
        ]

    def projected(features, columns):
        partial = jnp.dot(features, basis[:, columns], preferred_element_type=F32).astype(BF16)
        return [partial[: tokens // 2], partial[tokens // 2 :]]

    grads = out_grads[0]
    others_grads = sibling(grads)
    sums_0 = projected(features, slice(0, width))
    coming_0 = exchange(sums_0, 0)
    sums_1 = projected(after(features, *sums_0), slice(width, rank))
    parity = jnp.reshape(core, (1,)).astype(jnp.int32)
    mine = turn(parity, after(grads, *sums_1), owned)
    sums_0 = add(sums_0, [after(term, mine) for term in coming_0])
    for step in range(1, len(offsets) - 1):
        sums_0 = add(sums_0, exchange(sums_0, step))
    coming_0 = exchange(sums_0, len(offsets) - 1)
    coming_1 = exchange([after(half, *sums_0) for half in sums_1], 0)
    theirs = turn(parity, after(others_grads, *sums_0), owned)
    stacks = [mine, theirs]
    sums_0 = add(sums_0, [after(term, theirs) for term in coming_0])
    both_0 = sums_0 + [sibling(half) for half in sums_0]

    whole = slice(0, owned)
    leaving = gradient(stacks, both_0, ring_order[:1], [whole])
    arrived_0 = onward(leaving[0])
    others_0 = gradient([after(mine, *leaving), theirs], both_0, ring_order[1:])

    sums_1 = plus(sums_1, [after(term, others_0) for term in coming_1], 2)
    coming_1 = exchange(sums_1, 1)
    for hop in range(1, hops - 1):
        token = accumulate(after(arrived_0, sums_1), others_0, hop - 1, whole)
        arrived_0 = onward(token)
    sums_1 = add_pairs(sums_1, [after(term, token) for term in coming_1])
    for step in range(2, len(offsets)):
        sums_1 = add_pairs(sums_1, exchange(sums_1, step))
    both_1 = sums_1 + [sibling(half) for half in sums_1]
    token = accumulate(after(arrived_0, sums_1), others_0, hops - 2, whole)
    arrived_0 = onward(token)

    ends = [0, owned]
    if owned % 16 == 0:
        ends = [-(-owned * index // 48) * 16 for index in range(4)]
    parts = [slice(*pair) for pair in zip(ends, ends[1:])]
    count = len(parts)

    leaving = gradient([after(mine, token), theirs], both_1, ring_order[:1], parts)
    arrived = [onward(value) for value in leaving]
    others = gradient([after(mine, *leaving), theirs], both_1, ring_order[1:])

    held = ()

    def step_of(arrived, stack, rows, column):
        nonlocal held
        first_next, second_next, direction = adam(
            arrived, stack, hops - 1, rows, first_moment[0], second_moment[0], held, column
        )
        held = (first_next, second_next)
        return direction

    starts = []
    token = others
    stages = list(offsets)

    def spread(token):
        offset = stages.pop(0)
        starts.extend([across(after(piece, token), offset) for piece in starts])

    directions = []
    events = sorted((2 * hop + 1.5 * part, part, hop) for part in range(count) for hop in range(1, chips))
    for number, (_, part, hop) in enumerate(events):
        rows = parts[part]
        if number == 1:
            starts.append(step_of(after(arrived_0, token), others_0, whole, 0))
        if number in (1, 3, 5):
            token = [token, *starts]
            if stages:
                spread(token)
        if hop < hops:
            token = accumulate(after(arrived[part], token), others, hop - 1, rows)
            arrived[part] = onward(token)
            continue
        token = step_of(after(arrived[part], token), others, rows, width)
        sent = after(token, directions[part - 2]) if part > 1 else token
        directions.append([token] + [across(sent, offset) for offset in range(1, fsdp_count)])
    while stages:
        spread(token)

    update = ()
    for rows, pieces in zip(parts, directions):
        pieces = [after(pieces[0], token), *pieces[1:]]
        update = (expand(order, starts, pieces, rows, basis, update),)
    return (update[0][None], held[0][None], held[1][None])


def solution(mesh):
    in_specs = (
        P(None, "dp", "fsdp"),
        P(None, "dp", "fsdp"),
        P(None, "fsdp", None),
        P(None, ("fsdp", "dp"), None),
        P(None, ("fsdp", "dp"), None),
    )
    out_specs = (
        P(None, None, "dp", "fsdp"),
        P(None, ("fsdp", "dp"), None),
        P(None, ("fsdp", "dp"), None),
    )
    return jax.shard_map(local, mesh=mesh, in_specs=in_specs, out_specs=out_specs, check_vma=False)
```

```python
import functools

import jax
import jax.numpy as jnp
from jax import lax
from jax.experimental import pallas as pl
from jax.experimental.pallas import tpu as pltpu
from jax.sharding import PartitionSpec as P

beta_first = 0.9
beta_second = 0.999
adam_count = 100.0
epsilon = 1e-08

F32 = jnp.float32
BF16 = jnp.bfloat16
COST = pl.CostEstimate(flops=1024, bytes_accessed=1 << 20, transcendentals=0)
PARAMS = pltpu.CompilerParams(vmem_limit_bytes=58 * 1024 * 1024)
RING_PARAMS = pltpu.CompilerParams(vmem_limit_bytes=64 * 1024 * 1024)


def turn(core, grads, owned):
    tokens, columns = grads.shape
    chips = columns // (2 * owned)
    block = tokens // 4

    def kernel(core_ref, grads_ref, out_ref):
        for parity in range(2):

            @pl.when(core_ref[0] == parity)
            def _(parity=parity):
                for chip in range(chips):
                    begin = (2 * chip + parity) * owned
                    low = begin // 128 * 128
                    high = min(-(-(begin + owned) // 128) * 128, columns)
                    value = grads_ref[:, low:high].T
                    out_ref[chip] = value[begin - low : begin - low + owned]

    return pl.pallas_call(
        kernel,
        out_shape=jax.ShapeDtypeStruct((chips, owned, tokens), BF16),
        grid_spec=pltpu.PrefetchScalarGridSpec(
            num_scalar_prefetch=1,
            grid=(4,),
            in_specs=[pl.BlockSpec((block, columns), lambda i, core_ref: (i, 0))],
            out_specs=pl.BlockSpec((chips, owned, block), lambda i, core_ref: (0, 0, i)),
        ),
        compiler_params=PARAMS,
        cost_estimate=COST,
        name="turn",
    )(core, grads)


def plus(ones, twos, runs=1):
    rows, width = ones[0].shape
    count, size = len(ones), width // runs
    block = pl.BlockSpec((rows // 2, width), lambda i: (i, 0))

    def kernel(*refs):
        for index in range(count):
            total = (refs[index][...].astype(F32) + refs[count + index][...].astype(F32)).astype(BF16)
            for run in range(runs):
                refs[(2 + run) * count + index][...] = total[:, run * size : (run + 1) * size]

    return pl.pallas_call(
        kernel,
        grid=(2,),
        out_shape=[jax.ShapeDtypeStruct((rows, size), BF16)] * (count * runs),
        in_specs=[block] * (2 * count),
        out_specs=[pl.BlockSpec((rows // 2, size), lambda i: (i, 0))] * (count * runs),
        compiler_params=RING_PARAMS,
        cost_estimate=COST,
        name="plus",
    )(*ones, *twos)


def gradient(stacks, pieces, order, cuts=None):
    _, owned, tokens = stacks[0].shape
    rows, run = pieces[0].shape
    width = run * len(pieces) // 4
    count = order.shape[0]

    def kernel(order_ref, *refs):
        piece_refs = refs[: len(pieces)]
        stack_refs = refs[len(pieces) : len(pieces) + 2]
        out_refs, (whole_ref, held_ref, sems) = refs[len(pieces) + 2 : -3], refs[-3:]
        step = pl.program_id(0)

        def fetch(block, side):
            return pltpu.make_async_copy(
                stack_refs[side].at[order_ref[block]],
                held_ref.at[block, :, pl.ds(side * tokens, tokens)],
                sems.at[block, side],
            )

        @pl.when(step == 0)
        def _():
            for block in range(count):
                for side in range(2):
                    fetch(block, side).start()
            for index, piece_ref in enumerate(piece_refs):
                side, place = divmod(index, len(pieces) // 2)
                row, column = side * tokens + place % 2 * rows, place // 2 * run
                whole_ref[row : row + rows, column : column + run] = piece_ref[...]

        for side in range(2):
            fetch(step, side).wait()
        value = jnp.dot(held_ref[step], whole_ref[...], preferred_element_type=F32).astype(BF16)
        if cuts is None:
            out_refs[0][0] = value
        else:
            for out_ref, cut in zip(out_refs, cuts):
                out_ref[...] = value[cut]

    if cuts is None:
        out_shape = [jax.ShapeDtypeStruct((count, owned, width), BF16)]
        out_specs = [pl.BlockSpec((1, owned, width), lambda i, order_ref: (i, 0, 0))]
    else:
        out_shape = [jax.ShapeDtypeStruct((cut.stop - cut.start, width), BF16) for cut in cuts]
        out_specs = [pl.BlockSpec(out.shape, lambda i, order_ref: (0, 0)) for out in out_shape]
    results = pl.pallas_call(
        kernel,
        out_shape=out_shape,
        grid_spec=pltpu.PrefetchScalarGridSpec(
            num_scalar_prefetch=1,
            grid=(count,),
            in_specs=[pl.BlockSpec((rows, run), lambda i, order_ref: (0, 0))] * len(pieces)
            + [pl.BlockSpec(memory_space=pl.ANY)] * 2,
            out_specs=out_specs,
            scratch_shapes=[
                pltpu.VMEM((2 * tokens, width), BF16),
                pltpu.VMEM((count, owned, 2 * tokens), BF16),
                pltpu.SemaphoreType.DMA((count, 2)),
            ],
        ),
        compiler_params=RING_PARAMS,
        cost_estimate=COST,
        name="gradient",
    )(order, *pieces, *stacks)
    return results[0] if cuts is None else results


def part_of(stack, block, rows):
    shape = (pl.Element(1), pl.Element(rows.stop - rows.start), pl.Element(stack.shape[2]))
    return pl.BlockSpec(shape, lambda i: (block, rows.start, 0))


def accumulate(arrived, own, block, rows):
    def kernel(own_ref, arrived_ref, out_ref):
        out_ref[...] = (own_ref[0].astype(F32) + arrived_ref[...].astype(F32)).astype(BF16)

    return pl.pallas_call(
        kernel,
        grid=(1,),
        out_shape=jax.ShapeDtypeStruct(arrived.shape, BF16),
        in_specs=[part_of(own, block, rows), pl.BlockSpec(memory_space=pltpu.VMEM)],
        out_specs=pl.BlockSpec(memory_space=pltpu.VMEM),
        compiler_params=RING_PARAMS,
        cost_estimate=COST,
        name="accumulate",
    )(own, arrived)


def adam(arrived, stack, block, rows, first, second, held, column):
    owned, rank = first.shape
    height, width = arrived.shape

    def kernel(arrived_ref, stack_ref, first_ref, second_ref, *refs):
        first_out, second_out, direction_out = refs[-3:]
        grad_low = arrived_ref[...].astype(F32) + stack_ref[0].astype(F32)
        first_next = beta_first * first_ref[...] + (1.0 - beta_first) * grad_low
        second_next = beta_second * second_ref[...] + (1.0 - beta_second) * grad_low * grad_low
        first_out[...] = first_next
        second_out[...] = second_next
        bias_first = 1.0 - beta_first**adam_count
        bias_second = 1.0 - beta_second**adam_count
        direction = first_next / bias_first / (jnp.sqrt(second_next / bias_second) + epsilon)
        direction_out[...] = direction.astype(BF16)

    rectangle = pl.BlockSpec((pl.Element(height), pl.Element(width)), lambda i: (rows.start, column))
    return pl.pallas_call(
        kernel,
        grid=(1,),
        out_shape=[
            jax.ShapeDtypeStruct((owned, rank), F32),
            jax.ShapeDtypeStruct((owned, rank), F32),
            jax.ShapeDtypeStruct((height, width), BF16),
        ],
        in_specs=[pl.BlockSpec(memory_space=pltpu.VMEM), part_of(stack, block, rows), rectangle, rectangle]
        + [pl.BlockSpec(memory_space=pl.ANY)] * len(held),
        out_specs=[rectangle, rectangle, pl.BlockSpec((height, width), lambda i: (0, 0))],
        input_output_aliases={4 + index: index for index in range(len(held))},
        compiler_params=RING_PARAMS,
        cost_estimate=COST,
        name="adam",
    )(arrived, stack, first, second, *held)


def expand(targets, starts, rests, rows, basis, held):
    count = len(starts)
    owned, begin = starts[0].shape
    height, width = rests[0].shape
    features, rank = basis.shape
    block = min(512, features)

    def kernel(targets_ref, basis_ref, *refs):
        start_refs, rest_refs, (out_ref, whole_ref) = refs[:count], refs[count : 2 * count], refs[-2:]

        @pl.when(pl.program_id(0) == 0)
        def _():
            for index in range(count):
                here = slice(index * height, (index + 1) * height)
                whole_ref[here, :begin] = start_refs[index][...]
                whole_ref[here, begin:] = rest_refs[index][...]

        value = lax.dot_general(
            whole_ref[...], basis_ref[...], (((1,), (1,)), ((), ())), preferred_element_type=F32
        )
        for index in range(count):
            out_ref[targets_ref[index]] = value[index * height : (index + 1) * height]

    return pl.pallas_call(
        kernel,
        out_shape=jax.ShapeDtypeStruct((count, owned, features), F32),
        grid_spec=pltpu.PrefetchScalarGridSpec(
            num_scalar_prefetch=1,
            grid=(features // block,),
            in_specs=[pl.BlockSpec((block, rank), lambda i, targets_ref: (i, 0))]
            + [pl.BlockSpec((pl.Element(height), pl.Element(begin)), lambda i, targets_ref: (rows.start, 0))] * count
            + [pl.BlockSpec((height, width), lambda i, targets_ref: (0, 0))] * count
            + [pl.BlockSpec(memory_space=pl.ANY)] * len(held),
            out_specs=pl.BlockSpec(
                (pl.Element(count), pl.Element(height), pl.Element(block)),
                lambda i, targets_ref: (0, rows.start, i * block),
            ),
            scratch_shapes=[pltpu.VMEM((count * height, rank), BF16)],
        ),
        input_output_aliases={2 + 2 * count: 0} if held else {},
        compiler_params=RING_PARAMS,
        cost_estimate=COST,
        name="expand",
    )(targets, basis, *starts, *rests, *held)


def total_of(*terms):
    total = terms[0].astype(F32)
    for term in terms[1:]:
        total = total + term.astype(F32)
    return total.astype(BF16)


def after(value, *earlier):
    return lax.optimization_barrier((value, *jax.tree.leaves(earlier)))[0]


def local(activations, out_grads, projector, first_moment, second_moment):
    owned = first_moment.shape[1]
    features = activations[0]
    basis = projector[0]
    rank = basis.shape[1]
    tokens = features.shape[0]
    dp_count, fsdp_count = lax.axis_size("dp"), lax.axis_size("fsdp")
    dp, fsdp = lax.axis_index("dp"), lax.axis_index("fsdp")
    chips = dp_count // 2
    chip, core = dp // 2, dp % 2
    width = rank // 4

    offsets = [1 << bit for bit in range(fsdp_count.bit_length() - 1)]
    order = jnp.stack([fsdp ^ offset for offset in range(fsdp_count)]).astype(jnp.int32)
    hops = chips - 1
    ring_order = (chip - 1 - jnp.arange(chips, dtype=jnp.int32) + chips) % chips

    def across(value, offset):
        return lax.ppermute(value, "fsdp", [(index, index ^ offset) for index in range(fsdp_count)])

    def sibling(value):
        return lax.ppermute(value, "dp", [(index, index ^ 1) for index in range(dp_count)])

    def onward(value):
        return lax.ppermute(value, "dp", [(index, (index + 2) % dp_count) for index in range(dp_count)])

    def exchange(halves, step):
        return [across(half, offsets[step if index % 2 == 0 else -1 - step]) for index, half in enumerate(halves)]

    def add(halves, arrived):
        return [total_of(half, term) for half, term in zip(halves, arrived)]

    def add_pairs(pieces, arrived):
        return [
            total
            for index in range(0, len(pieces), 2)
            for total in plus(pieces[index : index + 2], arrived[index : index + 2])
        ]

    def projected(features, columns):
        partial = jnp.dot(features, basis[:, columns], preferred_element_type=F32).astype(BF16)
        return [partial[: tokens // 2], partial[tokens // 2 :]]

    grads = out_grads[0]
    others_grads = sibling(grads)
    sums_0 = projected(features, slice(0, width))
    coming_0 = exchange(sums_0, 0)
    sums_1 = projected(after(features, *sums_0), slice(width, rank))
    parity = jnp.reshape(core, (1,)).astype(jnp.int32)
    mine = turn(parity, after(grads, *sums_1), owned)
    sums_0 = add(sums_0, [after(term, mine) for term in coming_0])
    for step in range(1, len(offsets) - 1):
        sums_0 = add(sums_0, exchange(sums_0, step))
    coming_0 = exchange(sums_0, len(offsets) - 1)
    coming_1 = exchange([after(half, *sums_0) for half in sums_1], 0)
    theirs = turn(parity, after(others_grads, *sums_0), owned)
    stacks = [mine, theirs]
    sums_0 = add(sums_0, [after(term, theirs) for term in coming_0])
    both_0 = sums_0 + [sibling(half) for half in sums_0]

    whole = slice(0, owned)
    leaving = gradient(stacks, both_0, ring_order[:1], [whole])
    arrived_0 = onward(leaving[0])
    sums_1 = plus(sums_1, [after(term, *leaving) for term in coming_1], 2)
    coming_1 = exchange(sums_1, 1)
    others_0 = gradient([after(mine, *sums_1), theirs], both_0, ring_order[1:])
    token = others_0
    for hop in range(1, hops - 1):
        token = accumulate(after(arrived_0, token), others_0, hop - 1, whole)
        arrived_0 = onward(token)
    sums_1 = add_pairs(sums_1, [after(term, token) for term in coming_1])
    for step in range(2, len(offsets)):
        sums_1 = add_pairs(sums_1, exchange(sums_1, step))
    both_1 = sums_1 + [sibling(half) for half in sums_1]

    ends = [0, owned]
    if owned % 16 == 0:
        ends = [-(-owned * index // 48) * 16 for index in range(4)]
    parts = [slice(*pair) for pair in zip(ends, ends[1:])]
    count = len(parts)

    leaving = gradient(stacks, both_1, ring_order[:1], parts)
    arrived = [onward(value) for value in leaving]
    token = accumulate(after(arrived_0, *leaving), others_0, hops - 2, whole)
    arrived_0 = onward(token)
    others = gradient([after(mine, token), theirs], both_1, ring_order[1:])

    held = ()

    def step_of(arrived, stack, rows, column):
        nonlocal held
        first_next, second_next, direction = adam(
            arrived, stack, hops - 1, rows, first_moment[0], second_moment[0], held, column
        )
        held = (first_next, second_next)
        return direction

    starts = []
    token = others
    stages = list(offsets)

    def spread(token):
        offset = stages.pop(0)
        starts.extend([across(after(piece, token), offset) for piece in starts])

    directions = []
    events = sorted((2 * hop + 1.5 * part, part, hop) for part in range(count) for hop in range(1, chips))
    for number, (_, part, hop) in enumerate(events):
        rows = parts[part]
        if number == 1:
            starts.append(step_of(after(arrived_0, token), others_0, whole, 0))
        if number in (1, 3, 5):
            token = [token, *starts]
            if stages:
                spread(token)
        if hop < hops:
            token = accumulate(after(arrived[part], token), others, hop - 1, rows)
            arrived[part] = onward(token)
            continue
        token = step_of(after(arrived[part], token), others, rows, width)
        sent = after(token, directions[part - 2]) if part > 1 else token
        directions.append([token] + [across(sent, offset) for offset in range(1, fsdp_count)])
    while stages:
        spread(token)

    update = ()
    for rows, pieces in zip(parts, directions):
        pieces = [after(pieces[0], token), *pieces[1:]]
        update = (expand(order, starts, pieces, rows, basis, update),)
    return (update[0][None], held[0][None], held[1][None])


def solution(mesh):
    in_specs = (
        P(None, "dp", "fsdp"),
        P(None, "dp", "fsdp"),
        P(None, "fsdp", None),
        P(None, ("fsdp", "dp"), None),
        P(None, ("fsdp", "dp"), None),
    )
    out_specs = (
        P(None, None, "dp", "fsdp"),
        P(None, ("fsdp", "dp"), None),
        P(None, ("fsdp", "dp"), None),
    )
    return jax.shard_map(local, mesh=mesh, in_specs=in_specs, out_specs=out_specs, check_vma=False)
```

```python
import functools

import jax
import jax.numpy as jnp
from jax import lax
from jax.experimental import pallas as pl
from jax.experimental.pallas import tpu as pltpu
from jax.sharding import PartitionSpec as P

beta_first = 0.9
beta_second = 0.999
adam_count = 100.0
epsilon = 1e-08

F32 = jnp.float32
BF16 = jnp.bfloat16
COST = pl.CostEstimate(flops=1024, bytes_accessed=1 << 20, transcendentals=0)
PARAMS = pltpu.CompilerParams(vmem_limit_bytes=58 * 1024 * 1024)
RING_PARAMS = pltpu.CompilerParams(vmem_limit_bytes=64 * 1024 * 1024)


def turn(core, grads, owned):
    tokens, columns = grads.shape
    chips = columns // (2 * owned)
    block = tokens // 4

    def kernel(core_ref, grads_ref, out_ref):
        for parity in range(2):

            @pl.when(core_ref[0] == parity)
            def _(parity=parity):
                for chip in range(chips):
                    begin = (2 * chip + parity) * owned
                    low = begin // 128 * 128
                    high = min(-(-(begin + owned) // 128) * 128, columns)
                    value = grads_ref[:, low:high].T
                    out_ref[chip] = value[begin - low : begin - low + owned]

    return pl.pallas_call(
        kernel,
        out_shape=jax.ShapeDtypeStruct((chips, owned, tokens), BF16),
        grid_spec=pltpu.PrefetchScalarGridSpec(
            num_scalar_prefetch=1,
            grid=(4,),
            in_specs=[pl.BlockSpec((block, columns), lambda i, core_ref: (i, 0))],
            out_specs=pl.BlockSpec((chips, owned, block), lambda i, core_ref: (0, 0, i)),
        ),
        compiler_params=PARAMS,
        cost_estimate=COST,
        name="turn",
    )(core, grads)


def plus(ones, twos, runs=1):
    rows, width = ones[0].shape
    count, size = len(ones), width // runs
    block = pl.BlockSpec((rows // 2, width), lambda i: (i, 0))

    def kernel(*refs):
        for index in range(count):
            total = (refs[index][...].astype(F32) + refs[count + index][...].astype(F32)).astype(BF16)
            for run in range(runs):
                refs[(2 + run) * count + index][...] = total[:, run * size : (run + 1) * size]

    return pl.pallas_call(
        kernel,
        grid=(2,),
        out_shape=[jax.ShapeDtypeStruct((rows, size), BF16)] * (count * runs),
        in_specs=[block] * (2 * count),
        out_specs=[pl.BlockSpec((rows // 2, size), lambda i: (i, 0))] * (count * runs),
        compiler_params=RING_PARAMS,
        cost_estimate=COST,
        name="plus",
    )(*ones, *twos)


def gradient(stacks, pieces, order, begin, count, cuts=None):
    _, owned, tokens = stacks[0].shape
    rows, run = pieces[0].shape
    width = run * len(pieces) // 4

    def kernel(order_ref, *refs):
        piece_refs = refs[: len(pieces)]
        stack_refs = refs[len(pieces) : len(pieces) + 2]
        out_refs, (whole_ref, held_ref, sems) = refs[len(pieces) + 2 : -3], refs[-3:]
        step = pl.program_id(0)

        def fetch(block, side):
            return pltpu.make_async_copy(
                stack_refs[side].at[order_ref[begin + block]],
                held_ref.at[block, :, pl.ds(side * tokens, tokens)],
                sems.at[block, side],
            )

        @pl.when(step == 0)
        def _():
            for block in range(count):
                for side in range(2):
                    fetch(block, side).start()
            for index, piece_ref in enumerate(piece_refs):
                side, place = divmod(index, len(pieces) // 2)
                row, column = side * tokens + place % 2 * rows, place // 2 * run
                whole_ref[row : row + rows, column : column + run] = piece_ref[...]

        for side in range(2):
            fetch(step, side).wait()
        value = jnp.dot(held_ref[step], whole_ref[...], preferred_element_type=F32).astype(BF16)
        if cuts is None:
            out_refs[0][0] = value
        else:
            for out_ref, cut in zip(out_refs, cuts):
                out_ref[...] = value[cut]

    if cuts is None:
        out_shape = [jax.ShapeDtypeStruct((count, owned, width), BF16)]
        out_specs = [pl.BlockSpec((1, owned, width), lambda i, order_ref: (i, 0, 0))]
    else:
        out_shape = [jax.ShapeDtypeStruct((cut.stop - cut.start, width), BF16) for cut in cuts]
        out_specs = [pl.BlockSpec(out.shape, lambda i, order_ref: (0, 0)) for out in out_shape]
    results = pl.pallas_call(
        kernel,
        out_shape=out_shape,
        grid_spec=pltpu.PrefetchScalarGridSpec(
            num_scalar_prefetch=1,
            grid=(count,),
            in_specs=[pl.BlockSpec((rows, run), lambda i, order_ref: (0, 0))] * len(pieces)
            + [pl.BlockSpec(memory_space=pl.ANY)] * 2,
            out_specs=out_specs,
            scratch_shapes=[
                pltpu.VMEM((2 * tokens, width), BF16),
                pltpu.VMEM((count, owned, 2 * tokens), BF16),
                pltpu.SemaphoreType.DMA((count, 2)),
            ],
        ),
        compiler_params=RING_PARAMS,
        cost_estimate=COST,
        name="gradient",
    )(order, *pieces, *stacks)
    return results[0] if cuts is None else results


def part_of(stack, block, rows):
    shape = (pl.Element(1), pl.Element(rows.stop - rows.start), pl.Element(stack.shape[2]))
    return pl.BlockSpec(shape, lambda i: (block, rows.start, 0))


def accumulate(arrived, own, block, rows):
    def kernel(own_ref, arrived_ref, out_ref):
        out_ref[...] = (own_ref[0].astype(F32) + arrived_ref[...].astype(F32)).astype(BF16)

    return pl.pallas_call(
        kernel,
        grid=(1,),
        out_shape=jax.ShapeDtypeStruct(arrived.shape, BF16),
        in_specs=[part_of(own, block, rows), pl.BlockSpec(memory_space=pltpu.VMEM)],
        out_specs=pl.BlockSpec(memory_space=pltpu.VMEM),
        compiler_params=RING_PARAMS,
        cost_estimate=COST,
        name="accumulate",
    )(own, arrived)


def adam(arrived, stack, block, rows, first, second, held, column):
    owned, rank = first.shape
    height, width = arrived.shape

    def kernel(arrived_ref, stack_ref, first_ref, second_ref, *refs):
        first_out, second_out, direction_out = refs[-3:]
        grad_low = arrived_ref[...].astype(F32) + stack_ref[0].astype(F32)
        first_next = beta_first * first_ref[...] + (1.0 - beta_first) * grad_low
        second_next = beta_second * second_ref[...] + (1.0 - beta_second) * grad_low * grad_low
        first_out[...] = first_next
        second_out[...] = second_next
        bias_first = 1.0 - beta_first**adam_count
        bias_second = 1.0 - beta_second**adam_count
        direction = first_next / bias_first / (jnp.sqrt(second_next / bias_second) + epsilon)
        direction_out[...] = direction.astype(BF16)

    rectangle = pl.BlockSpec((pl.Element(height), pl.Element(width)), lambda i: (rows.start, column))
    return pl.pallas_call(
        kernel,
        grid=(1,),
        out_shape=[
            jax.ShapeDtypeStruct((owned, rank), F32),
            jax.ShapeDtypeStruct((owned, rank), F32),
            jax.ShapeDtypeStruct((height, width), BF16),
        ],
        in_specs=[pl.BlockSpec(memory_space=pltpu.VMEM), part_of(stack, block, rows), rectangle, rectangle]
        + [pl.BlockSpec(memory_space=pl.ANY)] * len(held),
        out_specs=[rectangle, rectangle, pl.BlockSpec((height, width), lambda i: (0, 0))],
        input_output_aliases={4 + index: index for index in range(len(held))},
        compiler_params=RING_PARAMS,
        cost_estimate=COST,
        name="adam",
    )(arrived, stack, first, second, *held)


def expand(targets, starts, rests, rows, basis, held):
    count = len(starts)
    owned, begin = starts[0].shape
    height, width = rests[0].shape
    features, rank = basis.shape
    block = min(512, features)

    def kernel(targets_ref, basis_ref, *refs):
        start_refs, rest_refs, (out_ref, whole_ref) = refs[:count], refs[count : 2 * count], refs[-2:]

        @pl.when(pl.program_id(0) == 0)
        def _():
            for index in range(count):
                here = slice(index * height, (index + 1) * height)
                whole_ref[here, :begin] = start_refs[index][...]
                whole_ref[here, begin:] = rest_refs[index][...]

        value = lax.dot_general(
            whole_ref[...], basis_ref[...], (((1,), (1,)), ((), ())), preferred_element_type=F32
        )
        for index in range(count):
            out_ref[targets_ref[index]] = value[index * height : (index + 1) * height]

    return pl.pallas_call(
        kernel,
        out_shape=jax.ShapeDtypeStruct((count, owned, features), F32),
        grid_spec=pltpu.PrefetchScalarGridSpec(
            num_scalar_prefetch=1,
            grid=(features // block,),
            in_specs=[pl.BlockSpec((block, rank), lambda i, targets_ref: (i, 0))]
            + [pl.BlockSpec((pl.Element(height), pl.Element(begin)), lambda i, targets_ref: (rows.start, 0))] * count
            + [pl.BlockSpec((height, width), lambda i, targets_ref: (0, 0))] * count
            + [pl.BlockSpec(memory_space=pl.ANY)] * len(held),
            out_specs=pl.BlockSpec(
                (pl.Element(count), pl.Element(height), pl.Element(block)),
                lambda i, targets_ref: (0, rows.start, i * block),
            ),
            scratch_shapes=[pltpu.VMEM((count * height, rank), BF16)],
        ),
        input_output_aliases={2 + 2 * count: 0} if held else {},
        compiler_params=RING_PARAMS,
        cost_estimate=COST,
        name="expand",
    )(targets, basis, *starts, *rests, *held)


def total_of(*terms):
    total = terms[0].astype(F32)
    for term in terms[1:]:
        total = total + term.astype(F32)
    return total.astype(BF16)


def after(value, *earlier):
    return lax.optimization_barrier((value, *jax.tree.leaves(earlier)))[0]


def local(activations, out_grads, projector, first_moment, second_moment):
    owned = first_moment.shape[1]
    features = activations[0]
    basis = projector[0]
    rank = basis.shape[1]
    tokens = features.shape[0]
    dp_count, fsdp_count = lax.axis_size("dp"), lax.axis_size("fsdp")
    dp, fsdp = lax.axis_index("dp"), lax.axis_index("fsdp")
    chips = dp_count // 2
    chip, core = dp // 2, dp % 2
    width = rank // 4

    offsets = [1 << bit for bit in range(fsdp_count.bit_length() - 1)]
    order = jnp.stack([fsdp ^ offset for offset in range(fsdp_count)]).astype(jnp.int32)
    hops = chips - 1
    ring_order = (chip - 1 - jnp.arange(chips, dtype=jnp.int32) + chips) % chips

    def across(value, offset):
        return lax.ppermute(value, "fsdp", [(index, index ^ offset) for index in range(fsdp_count)])

    def sibling(value):
        return lax.ppermute(value, "dp", [(index, index ^ 1) for index in range(dp_count)])

    def onward(value):
        return lax.ppermute(value, "dp", [(index, (index + 2) % dp_count) for index in range(dp_count)])

    def exchange(halves, step):
        return [across(half, offsets[step if index % 2 == 0 else -1 - step]) for index, half in enumerate(halves)]

    def add(halves, arrived):
        return [total_of(half, term) for half, term in zip(halves, arrived)]

    def add_pairs(pieces, arrived):
        return [
            total
            for index in range(0, len(pieces), 2)
            for total in plus(pieces[index : index + 2], arrived[index : index + 2])
        ]

    def projected(features, columns):
        partial = jnp.dot(features, basis[:, columns], preferred_element_type=F32).astype(BF16)
        return [partial[: tokens // 2], partial[tokens // 2 :]]

    grads = out_grads[0]
    others_grads = sibling(grads)
    sums_0 = projected(features, slice(0, width))
    coming_0 = exchange(sums_0, 0)
    later = after(features, *sums_0)
    sums_1 = [
        jnp.dot(half, basis[:, width:], preferred_element_type=F32).astype(BF16)
        for half in (later[: tokens // 2], later[tokens // 2 :])
    ]
    parity = jnp.reshape(core, (1,)).astype(jnp.int32)
    mine = turn(parity, after(grads, *sums_1), owned)
    sums_0 = add(sums_0, [after(term, mine) for term in coming_0])
    for step in range(1, len(offsets) - 1):
        sums_0 = add(sums_0, exchange(sums_0, step))
    coming_0 = exchange(sums_0, len(offsets) - 1)
    coming_1 = exchange([after(half, *sums_0) for half in sums_1], 0)
    theirs = turn(parity, after(others_grads, *sums_0), owned)
    stacks = [mine, theirs]
    sums_0 = add(sums_0, [after(term, theirs) for term in coming_0])
    both_0 = sums_0 + [sibling(half) for half in sums_0]

    whole = slice(0, owned)
    leaving = gradient(stacks, both_0, ring_order, 0, 1, [whole])
    arrived_0 = onward(leaving[0])
    sums_1 = plus(sums_1, [after(term, *leaving) for term in coming_1], 2)
    coming_1 = exchange(sums_1, 1)
    others_0 = gradient([after(mine, *sums_1), theirs], both_0, ring_order, 1, hops)
    token = others_0
    for hop in range(1, hops - 1):
        token = accumulate(after(arrived_0, token), others_0, hop - 1, whole)
        arrived_0 = onward(token)
    sums_1 = add_pairs(sums_1, [after(term, token) for term in coming_1])
    for step in range(2, len(offsets)):
        sums_1 = add_pairs(sums_1, exchange(sums_1, step))
    both_1 = sums_1 + [sibling(half) for half in sums_1]

    ends = [0, owned]
    if owned % 16 == 0:
        ends = [-(-owned * index // 48) * 16 for index in range(4)]
    parts = [slice(*pair) for pair in zip(ends, ends[1:])]
    count = len(parts)

    leaving = gradient(stacks, both_1, ring_order, 0, 1, parts)
    arrived = [onward(value) for value in leaving]
    token = accumulate(after(arrived_0, *leaving), others_0, hops - 2, whole)
    arrived_0 = onward(token)
    others = gradient([after(mine, token), theirs], both_1, ring_order, 1, hops)

    held = ()

    def step_of(arrived, stack, rows, column):
        nonlocal held
        first_next, second_next, direction = adam(
            arrived, stack, hops - 1, rows, first_moment[0], second_moment[0], held, column
        )
        held = (first_next, second_next)
        return direction

    starts = []
    token = others
    stages = list(offsets)

    def spread(token):
        offset = stages.pop(0)
        starts.extend([across(after(piece, token), offset) for piece in starts])

    directions = []
    events = sorted((2 * hop + 1.5 * part, part, hop) for part in range(count) for hop in range(1, chips))
    for number, (_, part, hop) in enumerate(events):
        rows = parts[part]
        if number == 0:
            token = [token, *arrived]
        if number == 2:
            starts.append(step_of(after(arrived_0, token), others_0, whole, 0))
        if number in (2, 4, 6):
            token = [token, *starts]
            if stages:
                spread(token)
        if hop < hops:
            token = accumulate(after(arrived[part], token), others, hop - 1, rows)
            arrived[part] = onward(token)
            continue
        token = step_of(after(arrived[part], token), others, rows, width)
        sent = after(token, directions[part - 2]) if part > 1 else token
        directions.append([token] + [across(sent, offset) for offset in range(1, fsdp_count)])
    while stages:
        spread(token)

    update = ()
    for rows, pieces in zip(parts, directions):
        pieces = [after(pieces[0], token), *pieces[1:]]
        update = (expand(order, starts, pieces, rows, basis, update),)
    return (update[0][None], held[0][None], held[1][None])


def solution(mesh):
    in_specs = (
        P(None, "dp", "fsdp"),
        P(None, "dp", "fsdp"),
        P(None, "fsdp", None),
        P(None, ("fsdp", "dp"), None),
        P(None, ("fsdp", "dp"), None),
    )
    out_specs = (
        P(None, None, "dp", "fsdp"),
        P(None, ("fsdp", "dp"), None),
        P(None, ("fsdp", "dp"), None),
    )
    return jax.shard_map(local, mesh=mesh, in_specs=in_specs, out_specs=out_specs, check_vma=False)
```

```python
import functools

import jax
import jax.numpy as jnp
from jax import lax
from jax.experimental import pallas as pl
from jax.experimental.pallas import tpu as pltpu
from jax.sharding import PartitionSpec as P

beta_first = 0.9
beta_second = 0.999
adam_count = 100.0
epsilon = 1e-08

F32 = jnp.float32
BF16 = jnp.bfloat16
COST = pl.CostEstimate(flops=1024, bytes_accessed=1 << 20, transcendentals=0)
PARAMS = pltpu.CompilerParams(vmem_limit_bytes=58 * 1024 * 1024)
RING_PARAMS = pltpu.CompilerParams(vmem_limit_bytes=64 * 1024 * 1024)


def turn(core, grads, owned):
    tokens, columns = grads.shape
    chips = columns // (2 * owned)
    block = tokens // 4

    def kernel(core_ref, grads_ref, out_ref):
        for parity in range(2):

            @pl.when(core_ref[0] == parity)
            def _(parity=parity):
                for chip in range(chips):
                    begin = (2 * chip + parity) * owned
                    low = begin // 128 * 128
                    high = min(-(-(begin + owned) // 128) * 128, columns)
                    value = grads_ref[:, low:high].T
                    out_ref[chip] = value[begin - low : begin - low + owned]

    return pl.pallas_call(
        kernel,
        out_shape=jax.ShapeDtypeStruct((chips, owned, tokens), BF16),
        grid_spec=pltpu.PrefetchScalarGridSpec(
            num_scalar_prefetch=1,
            grid=(4,),
            in_specs=[pl.BlockSpec((block, columns), lambda i, core_ref: (i, 0))],
            out_specs=pl.BlockSpec((chips, owned, block), lambda i, core_ref: (0, 0, i)),
        ),
        compiler_params=PARAMS,
        cost_estimate=COST,
        name="turn",
    )(core, grads)


def plus(ones, twos):
    rows, width = ones[0].shape
    count = len(ones)
    block = pl.BlockSpec((rows // 2, width), lambda i: (i, 0))

    def kernel(*refs):
        for one_ref, two_ref, out_ref in zip(refs, refs[count:], refs[2 * count :]):
            out_ref[...] = (one_ref[...].astype(F32) + two_ref[...].astype(F32)).astype(BF16)

    return pl.pallas_call(
        kernel,
        grid=(2,),
        out_shape=[jax.ShapeDtypeStruct((rows, width), BF16)] * count,
        in_specs=[block] * (2 * count),
        out_specs=[block] * count,
        compiler_params=RING_PARAMS,
        cost_estimate=COST,
        name="plus",
    )(*ones, *twos)


def gradient(stacks, pieces, order, cuts=None):
    _, owned, tokens = stacks[0].shape
    rows, width = pieces[0].shape
    count = order.shape[0]

    def kernel(order_ref, *refs):
        piece_refs = refs[: len(pieces)]
        stack_refs = refs[len(pieces) : len(pieces) + 2]
        out_refs, (whole_ref, held_ref, sems) = refs[len(pieces) + 2 : -3], refs[-3:]
        step = pl.program_id(0)

        def fetch(block, side):
            return pltpu.make_async_copy(
                stack_refs[side].at[order_ref[block]],
                held_ref.at[block, :, pl.ds(side * tokens, tokens)],
                sems.at[block, side],
            )

        @pl.when(step == 0)
        def _():
            for block in range(count):
                for side in range(2):
                    fetch(block, side).start()
            for index, piece_ref in enumerate(piece_refs):
                whole_ref[index * rows : (index + 1) * rows, :] = piece_ref[...]

        for side in range(2):
            fetch(step, side).wait()
        value = jnp.dot(held_ref[step], whole_ref[...], preferred_element_type=F32).astype(BF16)
        if cuts is None:
            out_refs[0][0] = value
        else:
            for out_ref, cut in zip(out_refs, cuts):
                out_ref[...] = value[cut]

    if cuts is None:
        out_shape = [jax.ShapeDtypeStruct((count, owned, width), BF16)]
        out_specs = [pl.BlockSpec((1, owned, width), lambda i, order_ref: (i, 0, 0))]
    else:
        out_shape = [jax.ShapeDtypeStruct((cut.stop - cut.start, width), BF16) for cut in cuts]
        out_specs = [pl.BlockSpec(out.shape, lambda i, order_ref: (0, 0)) for out in out_shape]
    results = pl.pallas_call(
        kernel,
        out_shape=out_shape,
        grid_spec=pltpu.PrefetchScalarGridSpec(
            num_scalar_prefetch=1,
            grid=(count,),
            in_specs=[pl.BlockSpec((rows, width), lambda i, order_ref: (0, 0))] * len(pieces)
            + [pl.BlockSpec(memory_space=pl.ANY)] * 2,
            out_specs=out_specs,
            scratch_shapes=[
                pltpu.VMEM((2 * tokens, width), BF16),
                pltpu.VMEM((count, owned, 2 * tokens), BF16),
                pltpu.SemaphoreType.DMA((count, 2)),
            ],
        ),
        compiler_params=RING_PARAMS,
        cost_estimate=COST,
        name="gradient",
    )(order, *pieces, *stacks)
    return results[0] if cuts is None else results


def part_of(stack, block, rows):
    shape = (pl.Element(1), pl.Element(rows.stop - rows.start), pl.Element(stack.shape[2]))
    return pl.BlockSpec(shape, lambda i: (block, rows.start, 0))


def accumulate(arrived, own, block, rows):
    def kernel(own_ref, arrived_ref, out_ref):
        out_ref[...] = (own_ref[0].astype(F32) + arrived_ref[...].astype(F32)).astype(BF16)

    return pl.pallas_call(
        kernel,
        grid=(1,),
        out_shape=jax.ShapeDtypeStruct(arrived.shape, BF16),
        in_specs=[part_of(own, block, rows), pl.BlockSpec(memory_space=pltpu.VMEM)],
        out_specs=pl.BlockSpec(memory_space=pltpu.VMEM),
        compiler_params=RING_PARAMS,
        cost_estimate=COST,
        name="accumulate",
    )(own, arrived)


def adam(arrived, stack, block, rows, first, second, held, column):
    owned, rank = first.shape
    height, width = arrived.shape

    def kernel(arrived_ref, stack_ref, first_ref, second_ref, *refs):
        first_out, second_out, direction_out = refs[-3:]
        grad_low = arrived_ref[...].astype(F32) + stack_ref[0].astype(F32)
        first_next = beta_first * first_ref[...] + (1.0 - beta_first) * grad_low
        second_next = beta_second * second_ref[...] + (1.0 - beta_second) * grad_low * grad_low
        first_out[...] = first_next
        second_out[...] = second_next
        bias_first = 1.0 - beta_first**adam_count
        bias_second = 1.0 - beta_second**adam_count
        direction = first_next / bias_first / (jnp.sqrt(second_next / bias_second) + epsilon)
        direction_out[...] = direction.astype(BF16)

    rectangle = pl.BlockSpec((pl.Element(height), pl.Element(width)), lambda i: (rows.start, column))
    return pl.pallas_call(
        kernel,
        grid=(1,),
        out_shape=[
            jax.ShapeDtypeStruct((owned, rank), F32),
            jax.ShapeDtypeStruct((owned, rank), F32),
            jax.ShapeDtypeStruct((height, width), BF16),
        ],
        in_specs=[pl.BlockSpec(memory_space=pltpu.VMEM), part_of(stack, block, rows), rectangle, rectangle]
        + [pl.BlockSpec(memory_space=pl.ANY)] * len(held),
        out_specs=[rectangle, rectangle, pl.BlockSpec((height, width), lambda i: (0, 0))],
        input_output_aliases={4 + index: index for index in range(len(held))},
        compiler_params=RING_PARAMS,
        cost_estimate=COST,
        name="adam",
    )(arrived, stack, first, second, *held)


def expand(targets, starts, rests, rows, basis, held):
    count = len(starts)
    owned, begin = starts[0].shape
    height, width = rests[0].shape
    features, rank = basis.shape
    block = min(512, features)

    def kernel(targets_ref, basis_ref, *refs):
        start_refs, rest_refs, (out_ref, whole_ref) = refs[:count], refs[count : 2 * count], refs[-2:]

        @pl.when(pl.program_id(0) == 0)
        def _():
            for index in range(count):
                here = slice(index * height, (index + 1) * height)
                whole_ref[here, :begin] = start_refs[index][...]
                whole_ref[here, begin:] = rest_refs[index][...]

        value = lax.dot_general(
            whole_ref[...], basis_ref[...], (((1,), (1,)), ((), ())), preferred_element_type=F32
        )
        for index in range(count):
            out_ref[targets_ref[index]] = value[index * height : (index + 1) * height]

    return pl.pallas_call(
        kernel,
        out_shape=jax.ShapeDtypeStruct((count, owned, features), F32),
        grid_spec=pltpu.PrefetchScalarGridSpec(
            num_scalar_prefetch=1,
            grid=(features // block,),
            in_specs=[pl.BlockSpec((block, rank), lambda i, targets_ref: (i, 0))]
            + [pl.BlockSpec((pl.Element(height), pl.Element(begin)), lambda i, targets_ref: (rows.start, 0))] * count
            + [pl.BlockSpec((height, width), lambda i, targets_ref: (0, 0))] * count
            + [pl.BlockSpec(memory_space=pl.ANY)] * len(held),
            out_specs=pl.BlockSpec(
                (pl.Element(count), pl.Element(height), pl.Element(block)),
                lambda i, targets_ref: (0, rows.start, i * block),
            ),
            scratch_shapes=[pltpu.VMEM((count * height, rank), BF16)],
        ),
        input_output_aliases={2 + 2 * count: 0} if held else {},
        compiler_params=RING_PARAMS,
        cost_estimate=COST,
        name="expand",
    )(targets, basis, *starts, *rests, *held)


def total_of(*terms):
    total = terms[0].astype(F32)
    for term in terms[1:]:
        total = total + term.astype(F32)
    return total.astype(BF16)


def after(value, *earlier):
    return lax.optimization_barrier((value, *jax.tree.leaves(earlier)))[0]


def local(activations, out_grads, projector, first_moment, second_moment):
    owned = first_moment.shape[1]
    features = activations[0]
    basis = projector[0]
    rank = basis.shape[1]
    tokens = features.shape[0]
    dp_count, fsdp_count = lax.axis_size("dp"), lax.axis_size("fsdp")
    dp, fsdp = lax.axis_index("dp"), lax.axis_index("fsdp")
    chips = dp_count // 2
    chip, core = dp // 2, dp % 2
    width = rank * 3 // 8

    offsets = [1 << bit for bit in range(fsdp_count.bit_length() - 1)]
    order = jnp.stack([fsdp ^ offset for offset in range(fsdp_count)]).astype(jnp.int32)
    hops = chips - 1
    ring_order = (chip - 1 - jnp.arange(chips, dtype=jnp.int32) + chips) % chips

    def across(value, offset):
        return lax.ppermute(value, "fsdp", [(index, index ^ offset) for index in range(fsdp_count)])

    def sibling(value):
        return lax.ppermute(value, "dp", [(index, index ^ 1) for index in range(dp_count)])

    def onward(value):
        return lax.ppermute(value, "dp", [(index, (index + 2) % dp_count) for index in range(dp_count)])

    def exchange(halves, step):
        return [across(half, offsets[step if index % 2 == 0 else -1 - step]) for index, half in enumerate(halves)]

    def add(halves, arrived):
        return [total_of(half, term) for half, term in zip(halves, arrived)]

    def projected(features, columns):
        partial = jnp.dot(features, basis[:, columns], preferred_element_type=F32).astype(BF16)
        return [partial[: tokens // 2], partial[tokens // 2 :]]

    grads = out_grads[0]
    others_grads = sibling(grads)
    sums_0 = projected(features, slice(0, width))
    coming_0 = exchange(sums_0, 0)
    later = after(features, *sums_0)
    sums_1 = [
        jnp.dot(half, basis[:, width:], preferred_element_type=F32).astype(BF16)
        for half in (later[: tokens // 2], later[tokens // 2 :])
    ]
    parity = jnp.reshape(core, (1,)).astype(jnp.int32)
    mine = turn(parity, after(grads, *sums_1), owned)
    sums_0 = add(sums_0, [after(term, mine) for term in coming_0])
    for step in range(1, len(offsets) - 1):
        sums_0 = add(sums_0, exchange(sums_0, step))
    coming_0 = exchange(sums_0, len(offsets) - 1)
    coming_1 = exchange([after(half, *sums_0) for half in sums_1], 0)
    theirs = turn(parity, after(others_grads, *sums_0), owned)
    stacks = [mine, theirs]
    sums_0 = add(sums_0, [after(term, theirs) for term in coming_0])
    both_0 = sums_0 + [sibling(half) for half in sums_0]

    whole = slice(0, owned)
    leaving = gradient(stacks, both_0, ring_order[:1], [whole])
    arrived_0 = onward(leaving[0])
    sums_1 = plus(sums_1, [after(term, *leaving) for term in coming_1])
    coming_1 = exchange(sums_1, 1)
    others_0 = gradient([after(mine, *sums_1), theirs], both_0, ring_order[1:])
    token = others_0
    for hop in range(1, hops - 1):
        token = accumulate(after(arrived_0, token), others_0, hop - 1, whole)
        arrived_0 = onward(token)
    sums_1 = plus(sums_1, [after(term, token) for term in coming_1])
    for step in range(2, len(offsets)):
        sums_1 = plus(sums_1, exchange(sums_1, step))
    both_1 = list(sums_1) + [sibling(half) for half in sums_1]

    ends = [0, owned]
    if owned % 16 == 0:
        ends = [-(-owned * index // 32) * 16 for index in range(3)]
    parts = [slice(*pair) for pair in zip(ends, ends[1:])]
    count = len(parts)

    leaving = gradient(stacks, both_1, ring_order[:1], parts)
    arrived = [onward(value) for value in leaving]
    others = gradient([after(mine, *leaving), theirs], both_1, ring_order[1:])
    token = accumulate(after(arrived_0, others), others_0, hops - 2, whole)
    arrived_0 = onward(token)

    held = ()

    def step_of(arrived, stack, rows, column):
        nonlocal held
        first_next, second_next, direction = adam(
            arrived, stack, hops - 1, rows, first_moment[0], second_moment[0], held, column
        )
        held = (first_next, second_next)
        return direction

    starts = []
    stages = list(offsets)

    def spread(token):
        offset = stages.pop(0)
        starts.extend([across(after(piece, token), offset) for piece in starts])

    directions = []
    events = sorted((2 * hop + 1.5 * part, part, hop) for part in range(count) for hop in range(1, chips))
    for number, (_, part, hop) in enumerate(events):
        rows = parts[part]
        if number == 0:
            token = [token, *arrived]
        if number == 2:
            starts.append(step_of(after(arrived_0, token), others_0, whole, 0))
        if number in (2, 4, 5):
            token = [token, *starts]
            if stages:
                spread(token)
        if hop < hops:
            token = accumulate(after(arrived[part], token), others, hop - 1, rows)
            arrived[part] = onward(token)
            continue
        token = step_of(after(arrived[part], token), others, rows, width)
        sent = after(token, directions[part - 2]) if part > 1 else token
        directions.append([token] + [across(sent, offset) for offset in range(1, fsdp_count)])
    while stages:
        spread(token)

    update = ()
    for rows, pieces in zip(parts, directions):
        pieces = [after(pieces[0], token), *pieces[1:]]
        update = (expand(order, starts, pieces, rows, basis, update),)
    return (update[0][None], held[0][None], held[1][None])


def solution(mesh):
    in_specs = (
        P(None, "dp", "fsdp"),
        P(None, "dp", "fsdp"),
        P(None, "fsdp", None),
        P(None, ("fsdp", "dp"), None),
        P(None, ("fsdp", "dp"), None),
    )
    out_specs = (
        P(None, None, "dp", "fsdp"),
        P(None, ("fsdp", "dp"), None),
        P(None, ("fsdp", "dp"), None),
    )
    return jax.shard_map(local, mesh=mesh, in_specs=in_specs, out_specs=out_specs, check_vma=False)
```
